32 devices in a mesh: dp: 4 (over y, core), ctx: 2 (over x), tp: 4 (over z).
Axes of the slice: x: 2, y: 2, z: 4, core: 2. Of those that a mesh axis runs over, the one named last changes fastest.
Arguments:
- hidden_in: bfloat16 [4, 5120, 1024], P('dp', ('ctx', 'tp')), may hold values from -6 to 6
- cotangent: bfloat16 [4, 5120, 1024], P('dp', ('ctx', 'tp')), may hold values from -6 to 6
- pic_starts: int32 [4, 4], P('dp'), may hold values from 0 to 4864, as said below
- norm_mixer: bfloat16 [1024], replicated, may hold values from 0.5 to 1.5
- w_query: bfloat16 [1024, 512], P(('dp', 'ctx'), 'tp'), may hold values from -0.1875 to 0.1875
- w_key: bfloat16 [1024, 512], P(('dp', 'ctx'), 'tp'), may hold values from -0.1875 to 0.1875
- w_value: bfloat16 [1024, 1024], P(('dp', 'ctx'), 'tp'), may hold values from -0.1875 to 0.1875
- w_outgate: bfloat16 [1024, 1024], P(('dp', 'ctx'), 'tp'), may hold values from -0.1875 to 0.1875
- w_rank_in: bfloat16 [1024, 16], replicated, may hold values from -0.1875 to 0.1875
- w_rank_out: bfloat16 [16, 512], replicated, may hold values from -1.5 to 1.5
- gate_bias: bfloat16 [512], replicated, may hold values from -2 to 6
- group_gain: bfloat16 [256], replicated, may hold values from 0.5 to 1.5
- w_output: bfloat16 [1024, 1024], P('tp', ('dp', 'ctx')), may hold values from -0.1875 to 0.1875
- norm_ffn: bfloat16 [1024], replicated, may hold values from 0.5 to 1.5
- w_gate: bfloat16 [1024, 2816], P(('dp', 'ctx'), 'tp'), may hold values from -0.1875 to 0.1875
- w_up: bfloat16 [1024, 2816], P(('dp', 'ctx'), 'tp'), may hold values from -0.1875 to 0.1875
- w_down: bfloat16 [2816, 1024], P('tp', ('dp', 'ctx')), may hold values from -0.109375 to 0.109375
Outputs:
- hidden_out: bfloat16 [4, 5120, 1024], P('dp', ('ctx', 'tp'))
- grad_in: float32 [4, 5120, 1024], P('dp', ('ctx', 'tp'))
- grad_norm_mixer: float32 [1024], replicated
- grad_query: float32 [1024, 512], P(('dp', 'ctx'), 'tp')
- grad_key: float32 [1024, 512], P(('dp', 'ctx'), 'tp')
- grad_value: float32 [1024, 1024], P(('dp', 'ctx'), 'tp')
- grad_outgate: float32 [1024, 1024], P(('dp', 'ctx'), 'tp')
- grad_rank_in: float32 [1024, 16], replicated
- grad_rank_out: float32 [16, 512], replicated
- grad_gate_bias: float32 [512], replicated
- grad_group_gain: float32 [256], replicated
- grad_output: float32 [1024, 1024], P('tp', ('dp', 'ctx'))
- grad_norm_ffn: float32 [1024], replicated
- grad_gate: float32 [1024, 2816], P(('dp', 'ctx'), 'tp')
- grad_up: float32 [1024, 2816], P(('dp', 'ctx'), 'tp')
- grad_down: float32 [2816, 1024], P('tp', ('dp', 'ctx'))
The draws below stay inside these ranges and needn't reach their ends.
Inputs may be any that keep to these rules, and one draw needn't show every extreme that they name: `pic_starts`: each row holds 4 different multiples of 256; a picture piece is the 256 tokens from its start on.
All inputs are finite; a program needn't handle non-finite values.
Results may differ from the reference program's by a relative error of at most 0.025.
Values may be sent and summed in bfloat16 or wider, within the bound.
No kernel may reach another device: no remote copies, remote signals or barrier semaphores. Data moves between devices by JAX's collectives and lax.ppermute only.
A program may use at most 256 MiB of HBM per device.

```python
import jax
import jax.numpy as jnp
from jax import lax

D = 1024
H = 4
DK = 128
DV = 256
RANK = 16
FF = 2816
SPAN = 64
PIECE = 256
NPIC = 4
LEN = 5120
BATCH = 4


def draw_pic_starts(key, part):
    block_total = LEN // PIECE
    row_keys = jax.random.split(key, BATCH)

    def pick_row(row_key):
        return jax.random.permutation(row_key, block_total)[:NPIC]
    chosen = jax.vmap(pick_row)(row_keys)
    return (chosen * PIECE).astype(jnp.int32)


def steps_of(key, dims, cuts, low, top_value):
    factor_of, own = 1.0, jax.random.fold_in(key, 6)
    for dim, shards_of in cuts:
        draws = jnp.exp(jax.random.uniform(jax.random.fold_in(own, dim), (shards_of,), jnp.float32, low / len(cuts), top_value / len(cuts)))
        factor_of = factor_of * jnp.repeat(draws, dims[dim] // shards_of).reshape([-1 if axis == dim else 1 for axis in range(len(dims))])
    return factor_of


def centred(stream_key, shape, spread, most, cuts=(), kind=jnp.bfloat16):
    factor_of = steps_of(stream_key, shape, cuts, -0.22, 0.18) if cuts else 1.0
    entries = jax.random.normal(stream_key, shape, jnp.float32) * spread * factor_of
    return jnp.minimum(jnp.maximum(entries, -most), most).astype(kind)


def setup_inputs(seed: int = 0) -> dict:
    key_list = jax.random.split(jax.random.key(seed), 18)
    return {
        "hidden_in": centred(key_list[0], (BATCH, LEN, D), 1.0, 6.0, ((0, 4), (1, 8))),
        "cotangent": centred(key_list[1], (BATCH, LEN, D), 1.0, 6.0, ((0, 4), (1, 8))),
        "pic_starts": draw_pic_starts(jax.random.fold_in(key_list[17], 71), 0),
        "norm_mixer": jnp.clip(1.0 + 0.1 * jax.random.normal(key_list[3], (D,), jnp.float32), 0.5, 1.5).astype(jnp.bfloat16),
        "w_query": centred(key_list[4], (D, H * DK), D ** -0.5, 0.1875, ((0, 8), (1, 4))),
        "w_key": centred(key_list[5], (D, H * DK), D ** -0.5, 0.1875, ((0, 8), (1, 4))),
        "w_value": centred(key_list[6], (D, H * DV), D ** -0.5, 0.1875, ((0, 8), (1, 4))),
        "w_outgate": centred(key_list[7], (D, H * DV), D ** -0.5, 0.1875, ((0, 8), (1, 4))),
        "w_rank_in": centred(key_list[8], (D, RANK), D ** -0.5, 0.1875),
        "w_rank_out": centred(key_list[9], (RANK, H * DK), RANK ** -0.5, 1.5),
        "gate_bias": jnp.clip(jax.random.uniform(key_list[10], (H * DK,), jnp.float32, -2.0, 6.0), -2.0, 6.0).astype(jnp.bfloat16),
        "group_gain": jnp.clip(1.0 + 0.1 * jax.random.normal(key_list[11], (DV,), jnp.float32), 0.5, 1.5).astype(jnp.bfloat16),
        "w_output": centred(key_list[12], (H * DV, D), (H * DV) ** -0.5, 0.1875, ((0, 4), (1, 8))),
        "norm_ffn": jnp.clip(1.0 + 0.1 * jax.random.normal(key_list[13], (D,), jnp.float32), 0.5, 1.5).astype(jnp.bfloat16),
        "w_gate": centred(key_list[14], (D, FF), D ** -0.5, 0.1875, ((0, 8), (1, 4))),
        "w_up": centred(key_list[15], (D, FF), D ** -0.5, 0.1875, ((0, 8), (1, 4))),
        "w_down": centred(key_list[16], (FF, D), FF ** -0.5, 0.109375, ((0, 4), (1, 8))),
    }


EPSILON = 1e-06
HIGHEST = lax.Precision.HIGHEST
GATE_NORM = 16.0

@jax.custom_vjp
def low(v):
    return lax.optimization_barrier(v.astype(jnp.bfloat16)).astype(jnp.float32)

@jax.custom_vjp
def low_back(v):
    return v

def low_keep(v):
    return (low(v), None)

def low_pass(kept, grad):
    return (grad,)

def back_keep(v):
    return (v, None)

def back_low(kept, grad):
    return (low(grad),)
low.defvjp(low_keep, low_pass)
low_back.defvjp(back_keep, back_low)

def block_causal(carried, inputs):
    queries, key_rows, value_rows, decays = inputs
    block_end = decays[-1]
    block_size = queries.shape[0]
    causal = (jnp.arange(block_size)[:, None] >= jnp.arange(block_size)[None, :]).astype(queries.dtype)
    query_decayed = queries * jnp.exp(decays)
    key_decayed = key_rows * jnp.exp(-decays)
    scores = jnp.einsum('thd,shd->hts', query_decayed, key_decayed, precision=HIGHEST) * causal
    within = jnp.einsum('hts,she->the', scores, value_rows, precision=HIGHEST)
    earlier = jnp.einsum('thd,hde->the', query_decayed, carried, precision=HIGHEST)
    key_final = key_rows * jnp.exp(block_end - decays)
    updated = jnp.exp(block_end)[:, :, None] * carried + jnp.einsum('thd,the->hde', key_final, value_rows, precision=HIGHEST)
    return (updated, within + earlier)

def block_future(carried, inputs):
    queries, key_rows, value_rows, decays, picture = inputs
    block_end = decays[-1]
    block_size = queries.shape[0]
    above = (jnp.arange(block_size)[:, None] < jnp.arange(block_size)[None, :]).astype(queries.dtype)
    query_decayed = queries * jnp.exp(-decays)
    key_decayed = key_rows * jnp.exp(decays)
    scores = jnp.einsum('thd,shd->hts', query_decayed, key_decayed, precision=HIGHEST) * above
    within = jnp.einsum('hts,she->the', scores, value_rows, precision=HIGHEST)
    later = jnp.einsum('thd,hde->the', queries * jnp.exp(block_end - decays), carried, precision=HIGHEST)
    updated = jnp.exp(block_end)[:, :, None] * carried + jnp.einsum('thd,the->hde', key_decayed, value_rows, precision=HIGHEST)
    return (updated, picture * (within + later))

def split_blocks(values):
    return values.reshape(values.shape[0] // SPAN, SPAN, *values.shape[1:])

def by_piece(values):
    group = PIECE // SPAN
    return values.reshape(values.shape[0] // group, group, *values.shape[1:])

def piece_future(start_state, scaled, key_blocks, value_blocks, decays, picture):

    def one_piece(piece_queries, piece_keys, piece_values, piece_decays, piece_mask):
        return lax.scan(jax.checkpoint(block_future), start_state, (piece_queries, piece_keys, piece_values, piece_decays, piece_mask), reverse=True)[1]
    future_out = jax.vmap(one_piece)(by_piece(scaled), by_piece(key_blocks), by_piece(value_blocks), by_piece(decays), by_piece(picture))
    return future_out.reshape(scaled.shape[0], *future_out.shape[2:])

def sequence_mixer(queries, key_rows, value_rows, gate_log, picture):
    scaled = split_blocks(queries * DK ** (-0.5))
    key_blocks = split_blocks(key_rows)
    value_blocks = split_blocks(value_rows)
    decays = jnp.cumsum(split_blocks(gate_log), axis=1)
    start_state = jnp.zeros((queries.shape[1], queries.shape[2], value_rows.shape[2]), queries.dtype)
    final_state, causal_out = lax.scan(jax.checkpoint(block_causal), start_state, (scaled, key_blocks, value_blocks, decays))
    future_out = piece_future(start_state, scaled, key_blocks, value_blocks, decays, picture)
    mixed = (causal_out + future_out).reshape(value_rows.shape)
    return (mixed, final_state, scaled, decays)

def matmul(left, right):
    return jnp.dot(left, right, precision=HIGHEST)

def rms_norm(values, gain):
    return values * lax.rsqrt(lax.optimization_barrier(jnp.mean(values * values, axis=-1, keepdims=True)) + EPSILON) * gain

def layer_forward(params, inputs, picture):
    norm_mixer, w_query, w_key, w_value, w_outgate, w_rank_in, w_rank_out, gate_bias, group_gain, w_output, norm_ffn, w_gate, w_up, w_down = params
    length = inputs.shape[0]
    normed = low(rms_norm(inputs, norm_mixer))
    queries = low_back(low(matmul(normed, w_query))).reshape(length, H, DK)
    key_rows = low_back(low(matmul(normed, w_key))).reshape(length, H, DK)
    value_rows = low_back(low(matmul(normed, w_value))).reshape(length, H, DV)
    outgate = low_back(matmul(normed, w_outgate)).reshape(length, H, DV)
    rank_low = low_back(low(matmul(normed, w_rank_in)))
    gate_in = low_back(matmul(rank_low, w_rank_out) + gate_bias)
    gate_log = (jax.nn.log_sigmoid(gate_in) / GATE_NORM).reshape(length, H, DK)
    mixed = sequence_mixer(queries, key_rows, value_rows, gate_log, picture)[0]
    grouped = rms_norm(mixed, group_gain)
    gated = low((grouped * outgate * jax.nn.sigmoid(outgate)).reshape(length, H * DV))
    residual = inputs + low_back(matmul(gated, w_output))
    normed_two = low(rms_norm(residual, norm_ffn))
    gate_pre = low_back(matmul(normed_two, w_gate))
    up_pre = low_back(matmul(normed_two, w_up))
    activation = low(gate_pre * jax.nn.sigmoid(gate_pre) * up_pre)
    return residual + matmul(activation, w_down)

def reference(hidden_in, cotangent, pic_starts, norm_mixer, w_query, w_key, w_value, w_outgate, w_rank_in, w_rank_out, gate_bias, group_gain, w_output, norm_ffn, w_gate, w_up, w_down):
    params = (norm_mixer.astype(jnp.float32), w_query.astype(jnp.float32), w_key.astype(jnp.float32), w_value.astype(jnp.float32), w_outgate.astype(jnp.float32), w_rank_in.astype(jnp.float32), w_rank_out.astype(jnp.float32), gate_bias.astype(jnp.float32), group_gain.astype(jnp.float32), w_output.astype(jnp.float32), norm_ffn.astype(jnp.float32), w_gate.astype(jnp.float32), w_up.astype(jnp.float32), w_down.astype(jnp.float32))
    block_count = LEN // SPAN
    positions = jnp.arange(block_count, dtype=jnp.int32) * SPAN

    def one_sequence(totals, sequence_item):
        inputs, upstream, starts = sequence_item
        inside = (positions[:, None] >= starts[None, :]) & (positions[:, None] < starts[None, :] + PIECE)
        picture = jnp.any(inside, axis=1).astype(jnp.float32)

        def forward(weights, values):
            return layer_forward(weights, values, picture)
        output, pullback = jax.vjp(forward, params, inputs.astype(jnp.float32))
        weight_grads, input_grad = pullback(upstream.astype(jnp.float32))
        totals = jax.tree.map(lambda summed, fresh: summed + fresh, totals, weight_grads)
        return (totals, (output.astype(jnp.bfloat16), input_grad))
    empty_grads = jax.tree.map(jnp.zeros_like, params)
    totals, (outputs, input_grads) = lax.scan(one_sequence, empty_grads, (hidden_in, cotangent, pic_starts))
    return (outputs, input_grads, totals[0], totals[1], totals[2], totals[3], totals[4], totals[5], totals[6], totals[7], totals[8], totals[9], totals[10], totals[11], totals[12], totals[13])
```

```python
import functools

import jax
import jax.numpy as jnp
from jax import lax
from jax.experimental import pallas as pl
from jax.experimental.pallas import tpu as pltpu
from jax.sharding import Mesh, PartitionSpec as P

DK = 128
DV = 256
RANK = 16
PIECE = 256
CHUNK = 128
EPSILON = 1e-06
GATE_NORM = 16.0
F32 = jnp.float32
BF16 = jnp.bfloat16
VMEM_LIMIT = 60 * 1024 * 1024


def nn(left, right):
    return lax.dot_general(left, right, (((1,), (0,)), ((), ())), preferred_element_type=F32)


def nt(left, right):
    return lax.dot_general(left, right, (((1,), (1,)), ((), ())), preferred_element_type=F32)


def tn(left, right):
    return lax.dot_general(left, right, (((0,), (0,)), ((), ())), preferred_element_type=F32)


def iota2(axis):
    return lax.broadcasted_iota(jnp.int32, (CHUNK, CHUNK), axis)


def split_dot(matrix, values, terms):
    total = None
    for _ in range(terms):
        part = values.astype(BF16)
        values = values - part.astype(F32)
        product = nn(matrix, part)
        total = product if total is None else total + product
    return total


def state_rows(state, log_decay):
    high = log_decay.astype(BF16).astype(F32)
    rows = lax.broadcasted_iota(jnp.int32, (16, DK), 0)
    extra = jnp.where(rows == 0, high, jnp.where(rows == 1, log_decay - high, 0.0))
    return jnp.concatenate([state, extra], axis=0).astype(BF16)


def states_kernel(chunks, qkv_ref, gate_ref, sums_ref, local_ref, future_ref, end_ref):
    lower = (iota2(0) >= iota2(1)).astype(BF16)
    state = jnp.zeros((DV, DK), F32)
    total = jnp.zeros((1, DK), F32)
    for j in range(chunks):
        rows = pl.ds(j * CHUNK, CHUNK)
        gate_in = gate_ref[rows, :]
        gate_log = (jnp.minimum(gate_in, 0.0) - jnp.log1p(jnp.exp(-jnp.abs(gate_in)))) * (
            1.0 / GATE_NORM
        )
        sums = split_dot(lower, gate_log, 3)
        sums_ref[rows, :] = sums
        last = sums[CHUNK - 1 : CHUNK, :]
        key_rows = qkv_ref[rows, DK : 2 * DK].astype(F32)
        value_rows = qkv_ref[rows, 2 * DK :]
        local_ref[0, j] = state
        both = jnp.concatenate(
            [(key_rows * jnp.exp(last - sums)).astype(BF16), (key_rows * jnp.exp(sums)).astype(BF16)],
            axis=1,
        )
        update = tn(value_rows, both)
        state = state * jnp.exp(last) + update[:, :DK]
        total = total + last
        future_ref[0, j] = update[:, DK:].astype(BF16)
    end_ref[0] = state_rows(state, total)


def scores_of(queries, key_rows, sums, pic):
    middle = sums[CHUNK // 2 - 1 : CHUNK // 2, :]
    grow = jnp.exp(sums - middle)
    shrink = jnp.exp(middle - sums)
    q1 = (queries * grow).astype(BF16)
    k1 = (key_rows * shrink).astype(BF16)
    q2 = (queries * shrink).astype(BF16)
    k2 = (key_rows * grow).astype(BF16)
    row, col = iota2(0), iota2(1)
    diagonal = jnp.sum(queries * key_rows, axis=1, keepdims=True)
    above = jnp.logical_and(row < col, pic > 0)
    scores = jnp.where(
        row > col,
        nt(q1, k1),
        jnp.where(row == col, diagonal, jnp.where(above, nt(q2, k2), 0.0)),
    )
    return scores, q1, k1, q2, k2, grow, shrink, above


def mix_kernel(
    chunks,
    flags_ref,
    qkv_ref,
    sums_ref,
    local_ref,
    incoming_ref,
    future_ref,
    later_ref,
    outgate_ref,
    gain_ref,
    mixed_ref,
    gated_ref,
):
    incoming = incoming_ref[0].astype(F32)
    before = jnp.zeros((1, DK), F32)
    gain = gain_ref[...]
    for j in range(chunks):
        rows = pl.ds(j * CHUNK, CHUNK)
        sums = sums_ref[rows, :]
        last = sums[CHUNK - 1 : CHUNK, :]
        queries = qkv_ref[rows, :DK].astype(F32) * DK**-0.5
        key_rows = qkv_ref[rows, DK : 2 * DK].astype(F32)
        value_rows = qkv_ref[rows, 2 * DK :]
        scores = scores_of(queries, key_rows, sums, flags_ref[0, j])[0]
        state = (local_ref[0, j] + incoming * jnp.exp(before)).astype(BF16)
        later = later_ref[0] if j == chunks - 1 else future_ref[0, j + 1]
        cross = flags_ref[1, j].astype(F32)
        factors = jnp.concatenate(
            [
                (queries * jnp.exp(sums)).astype(BF16),
                (queries * (jnp.exp(last - sums) * cross)).astype(BF16),
            ],
            axis=1,
        )
        mixed = nn(scores.astype(BF16), value_rows) + nt(
            factors, jnp.concatenate([state, later], axis=1)
        )
        before = before + last
        mixed_ref[rows, :] = mixed
        scale = lax.rsqrt(jnp.mean(mixed * mixed, axis=1, keepdims=True) + EPSILON)
        gate = outgate_ref[rows, :]
        gated_ref[rows, :] = (mixed * scale * gain * gate * jax.nn.sigmoid(gate)).astype(BF16)


def gate_back_kernel(
    chunks,
    flags_ref,
    d_gated_ref,
    outgate_ref,
    mixed_ref,
    gain_ref,
    qkv_ref,
    sums_ref,
    d_outgate_ref,
    d_mixed_ref,
    gain_grad_ref,
    local_ref,
    end_ref,
    earlier_ref,
):
    gain = gain_ref[...]
    state = jnp.zeros((DV, DK), F32)
    total = jnp.zeros((1, DK), F32)
    gain_grad = jnp.zeros((1, DV), F32)
    for j in reversed(range(chunks)):
        rows = pl.ds(j * CHUNK, CHUNK)
        d_gated = d_gated_ref[rows, :]
        gate = outgate_ref[rows, :]
        mixed = mixed_ref[rows, :]
        sigma = jax.nn.sigmoid(gate)
        scale = lax.rsqrt(jnp.mean(mixed * mixed, axis=1, keepdims=True) + EPSILON)
        unit = mixed * scale
        d_grouped = d_gated * gate * sigma
        slope = sigma * (1.0 + gate * (1.0 - sigma))
        d_outgate_ref[rows, :] = (d_gated * unit * gain * slope).astype(BF16)
        gain_grad = gain_grad + jnp.sum(d_grouped * unit, axis=0, keepdims=True)
        weighted = gain * d_grouped
        d_mixed = scale * (weighted - unit * jnp.mean(weighted * unit, axis=1, keepdims=True))
        d_low = d_mixed.astype(BF16)
        d_mixed_ref[rows, :] = d_low
        sums = sums_ref[rows, :]
        last = sums[CHUNK - 1 : CHUNK, :]
        queries = qkv_ref[rows, :DK].astype(F32) * DK**-0.5
        local_ref[0, j] = state
        update = tn(d_low, (queries * jnp.exp(sums)).astype(BF16))
        if j == chunks - 1:
            cross = flags_ref[1, j].astype(F32)
            earlier_ref[0] = tn(
                d_low, (queries * (jnp.exp(last - sums) * cross)).astype(BF16)
            ).astype(BF16)
        state = state * jnp.exp(last) + update
        total = total + last
    gain_grad_ref[0] = gain_grad
    end_ref[0] = state_rows(state, total)


def mix_back_kernel(
    chunks,
    flags_ref,
    d_mixed_ref,
    qkv_ref,
    sums_ref,
    local_ref,
    incoming_ref,
    future_ref,
    later_ref,
    back_local_ref,
    back_incoming_ref,
    earlier_ref,
    gate_ref,
    d_qkv_ref,
    d_gate_ref,
):
    incoming = incoming_ref[0].astype(F32)
    back_incoming = back_incoming_ref[0].astype(F32)
    lasts = [sums_ref[pl.ds(j * CHUNK + CHUNK - 1, 1), :] for j in range(chunks)]
    row, col = iota2(0), iota2(1)
    upper = (row <= col).astype(BF16)
    before = jnp.zeros((1, DK), F32)
    d_future = earlier_ref[0]
    for j in range(chunks):
        rows = pl.ds(j * CHUNK, CHUNK)
        sums = sums_ref[rows, :]
        last = lasts[j]
        after = jnp.zeros((1, DK), F32)
        for l in range(j + 1, chunks):
            after = after + lasts[l]
        queries = qkv_ref[rows, :DK].astype(F32) * DK**-0.5
        key_rows = qkv_ref[rows, DK : 2 * DK].astype(F32)
        value_rows = qkv_ref[rows, 2 * DK :]
        d_mixed = d_mixed_ref[rows, :]
        scores, q1, k1, q2, k2, grow, shrink, above = scores_of(
            queries, key_rows, sums, flags_ref[0, j]
        )
        state = local_ref[0, j] + incoming * jnp.exp(before)
        back_state = back_local_ref[0, j] + back_incoming * jnp.exp(after)
        later = later_ref[0] if j == chunks - 1 else future_ref[0, j + 1]
        cross = flags_ref[1, j].astype(F32)
        from_start = jnp.exp(sums)
        to_end = jnp.exp(last - sums)
        to_later = to_end * cross
        d_scores = nt(d_mixed, value_rows)
        on_diagonal = jnp.sum(jnp.where(row == col, d_scores, 0.0), axis=1, keepdims=True)
        below = jnp.where(row > col, d_scores, 0.0).astype(BF16)
        ahead = jnp.where(above, d_scores, 0.0).astype(BF16)
        dq_causal = grow * nn(below, k1)
        dk_causal = shrink * tn(below, q1)
        dq_ahead = shrink * nn(ahead, k2)
        dk_ahead = grow * tn(ahead, q2)
        d_factors = nn(d_mixed, jnp.concatenate([state.astype(BF16), later], axis=1))
        dq_causal = dq_causal + from_start * d_factors[:, :DK]
        dq_later = to_later * d_factors[:, DK:]
        back_pair = jnp.concatenate([back_state.astype(BF16), d_future], axis=1)
        d_factors = nn(value_rows, back_pair)
        dk_state = to_end * d_factors[:, :DK]
        dk_earlier = from_start * d_factors[:, DK:]
        key_factors = jnp.concatenate(
            [(key_rows * to_end).astype(BF16), (key_rows * from_start).astype(BF16)], axis=1
        )
        d_values = tn(scores.astype(BF16), d_mixed) + nt(key_factors, back_pair)
        d_future = tn(d_mixed, (queries * to_later).astype(BF16)).astype(BF16)
        d_sums = queries * (dq_causal - dq_ahead - dq_later) + key_rows * (
            dk_ahead + dk_earlier - dk_causal - dk_state
        )
        d_last = (
            jnp.sum(key_rows * dk_state + queries * dq_later, axis=0, keepdims=True)
            + jnp.sum(state * back_state, axis=0, keepdims=True) * jnp.exp(last)
        )
        d_log = split_dot(upper, d_sums, 2) + d_last
        gate_in = gate_ref[rows, :]
        d_gate_ref[rows, :] = (d_log * jax.nn.sigmoid(-gate_in) * (1.0 / GATE_NORM)).astype(BF16)
        d_qkv_ref[rows, :DK] = (
            (dq_causal + dq_ahead + dq_later + on_diagonal * key_rows) * DK**-0.5
        ).astype(BF16)
        d_qkv_ref[rows, DK : 2 * DK] = (
            dk_causal + dk_ahead + dk_state + dk_earlier + on_diagonal * queries
        ).astype(BF16)
        d_qkv_ref[rows, 2 * DK :] = d_values.astype(BF16)
        before = before + last


def rows_block(length, width):
    return pl.BlockSpec((length, width), lambda h: (0, h))


def lead_block(*inner):
    return pl.BlockSpec((1, *inner), lambda h: (h,) + (0,) * len(inner))


def whole_block(*dims):
    return pl.BlockSpec(dims, lambda h: (0,) * len(dims))


def smem():
    return pl.BlockSpec(memory_space=pltpu.SMEM)


def params():
    return pltpu.CompilerParams(vmem_limit_bytes=VMEM_LIMIT)


def shaped(shape, kind):
    return jax.ShapeDtypeStruct(shape, kind)


def chunk_states(qkv, gate_in, heads):
    length = qkv.shape[0]
    chunks = length // CHUNK
    width = 2 * DK + DV
    return pl.pallas_call(
        functools.partial(states_kernel, chunks),
        grid=(heads,),
        in_specs=[rows_block(length, width), rows_block(length, DK)],
        out_specs=[
            rows_block(length, DK),
            lead_block(chunks, DV, DK),
            lead_block(chunks, DV, DK),
            lead_block(DV + 16, DK),
        ],
        out_shape=[
            shaped((length, heads * DK), F32),
            shaped((heads, chunks, DV, DK), F32),
            shaped((heads, chunks, DV, DK), BF16),
            shaped((heads, DV + 16, DK), BF16),
        ],
        compiler_params=params(),
        name="chunk_states",
    )(qkv, gate_in)


def mix(flags, qkv, sums, local, incoming, future, later, outgate, gain):
    length = qkv.shape[0]
    heads, chunks = local.shape[:2]
    width = 2 * DK + DV
    return pl.pallas_call(
        functools.partial(mix_kernel, chunks),
        grid=(heads,),
        in_specs=[
            smem(),
            rows_block(length, width),
            rows_block(length, DK),
            lead_block(chunks, DV, DK),
            lead_block(DV, DK),
            lead_block(chunks, DV, DK),
            lead_block(DV, DK),
            rows_block(length, DV),
            whole_block(1, DV),
        ],
        out_specs=[rows_block(length, DV), rows_block(length, DV)],
        out_shape=[shaped((length, heads * DV), F32), shaped((length, heads * DV), BF16)],
        compiler_params=params(),
        name="mix",
    )(flags, qkv, sums, local, incoming, future, later, outgate, gain)


def gate_back(flags, d_gated, outgate, mixed, gain, qkv, sums, heads):
    length = qkv.shape[0]
    chunks = length // CHUNK
    width = 2 * DK + DV
    return pl.pallas_call(
        functools.partial(gate_back_kernel, chunks),
        grid=(heads,),
        in_specs=[
            smem(),
            rows_block(length, DV),
            rows_block(length, DV),
            rows_block(length, DV),
            whole_block(1, DV),
            rows_block(length, width),
            rows_block(length, DK),
        ],
        out_specs=[
            rows_block(length, DV),
            rows_block(length, DV),
            lead_block(1, DV),
            lead_block(chunks, DV, DK),
            lead_block(DV + 16, DK),
            lead_block(DV, DK),
        ],
        out_shape=[
            shaped((length, heads * DV), BF16),
            shaped((length, heads * DV), BF16),
            shaped((heads, 1, DV), F32),
            shaped((heads, chunks, DV, DK), F32),
            shaped((heads, DV + 16, DK), BF16),
            shaped((heads, DV, DK), BF16),
        ],
        compiler_params=params(),
        name="gate_back",
    )(flags, d_gated, outgate, mixed, gain, qkv, sums)


def mix_back(
    flags, d_mixed, qkv, sums, local, incoming, future, later, back_local, back_incoming, earlier, gate_in
):
    length = qkv.shape[0]
    heads, chunks = local.shape[:2]
    width = 2 * DK + DV
    return pl.pallas_call(
        functools.partial(mix_back_kernel, chunks),
        grid=(heads,),
        in_specs=[
            smem(),
            rows_block(length, DV),
            rows_block(length, width),
            rows_block(length, DK),
            lead_block(chunks, DV, DK),
            lead_block(DV, DK),
            lead_block(chunks, DV, DK),
            lead_block(DV, DK),
            lead_block(chunks, DV, DK),
            lead_block(DV, DK),
            lead_block(DV, DK),
            rows_block(length, DK),
        ],
        out_specs=[rows_block(length, width), rows_block(length, DK)],
        out_shape=[shaped((length, heads * width), BF16), shaped((length, heads * DK), BF16)],
        compiler_params=params(),
        name="mix_back",
    )(
        flags, d_mixed, qkv, sums, local, incoming, future, later, back_local, back_incoming, earlier, gate_in
    )


def chain_kernel(count, backwards, place_ref, *refs):
    parts, other_ref, total_ref = refs[:count], refs[count], refs[count + 1]
    outs, scratch, result = refs[count + 2 : 2 * count + 2], refs[-2], refs[-1]
    place, joined = place_ref[0], place_ref[1]
    for k in range(count):
        scratch[lax.rem(place + k, count)] = parts[k][...].astype(F32)
    state = jnp.where(joined > 0, other_ref[:DV, :].astype(F32), 0.0)
    for z in reversed(range(count)) if backwards else range(count):
        result[z] = state.astype(BF16)
        log_decay = scratch[z, DV : DV + 1, :] + scratch[z, DV + 1 : DV + 2, :]
        state = state * jnp.exp(log_decay) + scratch[z, :DV, :]
    total_ref[...] = state.astype(BF16)
    for k in range(count):
        outs[k][...] = result[lax.rem(place + k, count)]


def chain(parts, other, place, joined, backwards):
    count = len(parts)
    return pl.pallas_call(
        functools.partial(chain_kernel, count, backwards),
        in_specs=[smem()] + [pl.BlockSpec(memory_space=pltpu.VMEM)] * (count + 1),
        out_specs=[pl.BlockSpec(memory_space=pltpu.VMEM)] * (count + 1),
        out_shape=[shaped((DV, DK), BF16)] * (count + 1),
        scratch_shapes=[
            pltpu.VMEM((count, DV + 16, DK), F32),
            pltpu.VMEM((count, DV, DK), BF16),
        ],
        compiler_params=params(),
        name="chain",
    )(jnp.stack([place, joined]).astype(jnp.int32), *parts, other)


def shifted(array, axis, by):
    size = lax.axis_size(axis)
    return lax.ppermute(array, axis, [(i, (i + by) % size) for i in range(size)])


def swapped(array, axis):
    return lax.ppermute(array, axis, [(0, 1), (1, 0)])


def exchange_states(ends, backwards):
    count = lax.axis_size("tp")
    place = lax.axis_index("tp")
    side = lax.axis_index("ctx")
    parts = [ends[0]] + [shifted(ends[k], "tp", -k) for k in range(1, count)]
    zero = jnp.zeros((DV, DK), BF16)
    total = chain(parts, zero, place, jnp.zeros_like(place), backwards)[0]
    other = swapped(total, "ctx")
    joined = (side == 0) if backwards else (side == 1)
    outs = chain(parts, other, place, joined.astype(place.dtype), backwards)[1:]
    return jnp.stack([outs[0]] + [shifted(outs[k], "tp", k) for k in range(1, count)])


def neighbour_future(first, odd_to_even):
    size = lax.axis_size("tp")
    if odd_to_even:
        moved = lax.ppermute(first, "tp", [(i + 1, i) for i in range(0, size - 1, 2)])
        return jnp.concatenate([moved[1:], moved[:1]], axis=0)
    moved = lax.ppermute(first, "tp", [(i, i + 1) for i in range(0, size - 1, 2)])
    return jnp.concatenate([moved[-1:], moved[:-1]], axis=0)


def split_axes():
    return all(lax.axis_size(axis) == 2 for axis in ("dpo", "core", "ctx"))


def column_order(back):
    if not split_axes():
        return None
    y, core, x = (lax.axis_index(axis) for axis in ("dpo", "core", "ctx"))
    order = []
    for j in range(8):
        high, middle, last = j >> 2, (j >> 1) & 1, j & 1
        if back:
            order.append(((core ^ middle) * 2 + (y ^ high)) * 2 + (x ^ last))
        else:
            order.append(((y ^ middle) * 2 + (core ^ high)) * 2 + (x ^ last))
    return order


def reorder(array, axis, back=False):
    order = column_order(back)
    if order is None:
        return array
    size = array.shape[axis] // len(order)
    return jnp.concatenate(
        [lax.dynamic_slice_in_dim(array, block * size, size, axis) for block in order], axis=axis
    )


def weight_axes(first):
    return ("ctx", "dpo") if first == "ctx" else ("dpo", "ctx")


def gather_weights(shards, first):
    count = lax.axis_size("tp")
    if not split_axes():
        place = lax.axis_index("tp")
        out = []
        for shard in shards:
            wide = lax.all_gather(shard, ("dpo", "core", "ctx"), axis=1, tiled=True)
            every = lax.all_gather(wide, "tp")
            every = jnp.take(every, lax.rem(place - jnp.arange(count) + count, count), axis=0)
            out.append(every.reshape(-1, every.shape[-1]))
        return jnp.concatenate(out, axis=0)
    one, two = weight_axes(first)
    shard = jnp.concatenate(shards, axis=0)
    slots = [shard] + [shifted(shard, "tp", k) for k in range(1, count)]
    rows, at = [], 0
    for part in shards:
        rows += [slot[at : at + part.shape[0]] for slot in slots]
        at += part.shape[0]
    pieces = {(0, 0): jnp.concatenate(rows, axis=0)}
    pieces[1, 0] = swapped(pieces[0, 0], one)
    pieces[0, 1] = swapped(pieces[0, 0], two)
    pieces[1, 1] = swapped(pieces[1, 0], two)
    own = [pieces[(y, x) if one == "dpo" else (x, y)] for y in (0, 1) for x in (0, 1)]
    return jnp.concatenate(own + [swapped(piece, "core") for piece in own], axis=1)


def scatter_grads(left, right, sizes, first):
    count = lax.axis_size("tp")
    if not split_axes():
        place = lax.axis_index("tp")
        whole = tn(left, right)
        out, at = [], 0
        for size in sizes:
            part = whole[at : at + count * size].reshape(count, size, -1)
            part = jnp.take(part, lax.rem(place - jnp.arange(count) + count, count), axis=0)
            part = lax.psum_scatter(part, "tp", scatter_dimension=0, tiled=True)[0]
            out.append(lax.psum_scatter(part, ("dpo", "core", "ctx"), scatter_dimension=1, tiled=True))
            at += count * size
        return out
    half = right.shape[1] // 2
    quarter = half // 4
    far = swapped(tn(left, right[:, half:]).astype(BF16), "core")
    near = tn(left, right[:, :half]) + far.astype(F32)
    blocks = {(i >> 1, i & 1): near[:, i * quarter : (i + 1) * quarter] for i in range(4)}
    if first == "ctx":
        blocks = {(x, y): block for (y, x), block in blocks.items()}
    one, two = weight_axes(first)
    sent = jnp.concatenate([blocks[1, 0], blocks[1, 1]], axis=1).astype(BF16)
    kept = jnp.concatenate([blocks[0, 0], blocks[0, 1]], axis=1).astype(BF16)
    sums = kept.astype(F32) + swapped(sent, one).astype(F32)
    sent, kept = sums[:, quarter:].astype(BF16), sums[:, :quarter].astype(BF16)
    sums = (kept.astype(F32) + swapped(sent, two).astype(F32)).astype(BF16)
    slots, at = [[] for _ in range(count)], 0
    for size in sizes:
        for k in range(count):
            slots[k].append(sums[at + k * size : at + (k + 1) * size])
        at += count * size
    slots = [jnp.concatenate(slot, axis=0) if len(slot) > 1 else slot[0] for slot in slots]
    total = slots[0].astype(F32)
    for k in range(1, count):
        total = total + shifted(slots[k], "tp", -k).astype(F32)
    out, at = [], 0
    for size in sizes:
        out.append(total[at : at + size])
        at += size
    return out


def sum_everywhere(values):
    if not split_axes() or lax.axis_size("tp") != 4:
        return lax.psum(values, ("dpo", "core", "ctx", "tp"))
    for axis in ("core", "ctx", "dpo"):
        values = values + swapped(values, axis)
    for pairs in ([(0, 1), (1, 0), (2, 3), (3, 2)], [(0, 2), (2, 0), (1, 3), (3, 1)]):
        values = values + lax.ppermute(values, "tp", pairs)
    return values


def rms_scale(values):
    return lax.rsqrt(jnp.mean(values * values, axis=-1, keepdims=True) + EPSILON)


def norm_back(upstream, values, scale, gain):
    weighted = upstream * gain
    return scale * weighted - values * scale**3 * jnp.mean(
        weighted * values, axis=-1, keepdims=True
    )


def on_device(
    hidden_in,
    cotangent,
    pic_starts,
    norm_mixer,
    w_query,
    w_key,
    w_value,
    w_outgate,
    w_rank_in,
    w_rank_out,
    gate_bias,
    group_gain,
    w_output,
    norm_ffn,
    w_gate,
    w_up,
    w_down,
):
    seq_count, length, model_width = hidden_in.shape
    assert seq_count == 1
    heads = lax.axis_size("tp")
    place = lax.axis_index("tp")
    chunks = length // CHUNK
    units = w_down.shape[0]
    half = units // 2

    cut = lambda array, index: array[index * half : (index + 1) * half]
    w_gate_t, w_up_t = w_gate.T, w_up.T
    w_in = jnp.concatenate([w_query.T, w_key.T, w_value.T], axis=0)
    w_in_all = gather_weights([w_in], "dpo")
    w_side_all = gather_weights([w_outgate.T, w_output], "ctx")
    w_og_all, w_out_all = w_side_all[: heads * DV], w_side_all[heads * DV :]
    ffn_all = [
        gather_weights([cut(w_gate_t, s), cut(w_up_t, s), cut(w_down, s)], ("dpo", "ctx")[s])
        for s in range(2)
    ]
    wide = heads * half

    head_order = lax.rem(place - jnp.arange(heads) + heads, heads)
    rank_out = jnp.take(w_rank_out.reshape(RANK, heads, DK), head_order, axis=1).reshape(
        RANK, heads * DK
    )
    bias = jnp.take(gate_bias.reshape(heads, DK), head_order, axis=0).reshape(heads * DK)
    rank_in = reorder(w_rank_in, 0)
    gain_one = reorder(norm_mixer, 0).astype(F32)
    gain_two = reorder(norm_ffn, 0).astype(F32)

    inputs_low = reorder(hidden_in[0], 1)
    upstream = reorder(cotangent[0], 1)
    inputs = inputs_low.astype(F32)
    scale_one = rms_scale(inputs)
    normed = (inputs * scale_one * gain_one).astype(BF16)

    part = lax.axis_index("ctx") * heads + place
    starts = part * length + jnp.arange(chunks, dtype=jnp.int32) * CHUNK
    inside = (starts[:, None] >= pic_starts[0][None, :]) & (
        starts[:, None] < pic_starts[0][None, :] + PIECE
    )
    in_piece = jnp.any(inside, axis=1)
    first_half = (starts % PIECE) == 0
    flags = jnp.stack([in_piece, in_piece & first_half]).astype(jnp.int32)

    qkv = nt(normed, w_in_all).astype(BF16)
    rank_low = nn(normed, rank_in).astype(BF16)
    gate_in = nn(rank_low, rank_out) + bias.astype(F32)
    sums, local, future, ends = chunk_states(qkv, gate_in, heads)
    later = neighbour_future(future[:, 0], True)
    incoming = exchange_states(ends, False)
    outgate = nt(normed, w_og_all)
    gain_group = group_gain.astype(F32)[None, :]
    mixed, gated = mix(flags, qkv, sums, local, incoming, future, later, outgate, gain_group)
    resid = inputs + nn(gated, w_out_all)
    scale_two = rms_scale(resid)
    normed_two = (resid * scale_two * gain_two).astype(BF16)

    feed = jnp.zeros_like(resid)
    d_norm_two = jnp.zeros_like(resid)
    grads = []
    for s in range(2):
        weights = ffn_all[s]
        gate_w, up_w, down_w = weights[:wide], weights[wide : 2 * wide], weights[2 * wide :]
        gate_pre, up_pre = nt(normed_two, gate_w), nt(normed_two, up_w)
        sigma = jax.nn.sigmoid(gate_pre)
        silu = gate_pre * sigma
        activation = (silu * up_pre).astype(BF16)
        feed = feed + nn(activation, down_w)
        d_act = nt(upstream, down_w)
        d_gate = (d_act * up_pre * (sigma * (1.0 + gate_pre * (1.0 - sigma)))).astype(BF16)
        d_up = (d_act * silu).astype(BF16)
        d_norm_two = d_norm_two + nn(d_gate, gate_w) + nn(d_up, up_w)
        order = ("ctx", "dpo")[s]
        grad_down = scatter_grads(activation, upstream, [half], order)[0]
        grad_gate = scatter_grads(d_gate, normed_two, [half], order)[0]
        grad_up = scatter_grads(d_up, normed_two, [half], order)[0]
        grads.append((grad_gate, grad_up, grad_down))
    hidden_out = reorder((resid + feed).astype(BF16), 1, True)[None]
    grad_gate, grad_up, grad_down = (jnp.concatenate(pair, axis=0) for pair in zip(*grads))

    grad_ffn_term = jnp.sum(d_norm_two * resid * scale_two, axis=0)
    d_resid = upstream.astype(F32) + norm_back(d_norm_two, resid, scale_two, gain_two)
    d_branch = d_resid.astype(BF16)
    d_gated = nt(d_branch, w_out_all)
    d_outgate, d_mixed, gain_terms, back_local, back_ends, earlier = gate_back(
        flags, d_gated, outgate, mixed, gain_group, qkv, sums, heads
    )
    grad_group_term = jnp.sum(gain_terms, axis=(0, 1))
    earlier = neighbour_future(earlier, False)
    back_incoming = exchange_states(back_ends, True)
    grad_output = scatter_grads(gated, d_branch, [DV], "ctx")[0]
    grad_outgate = scatter_grads(d_outgate, normed, [DV], "dpo")[0]
    d_qkv, d_gate_in = mix_back(
        flags, d_mixed, qkv, sums, local, incoming, future, later, back_local, back_incoming, earlier, gate_in
    )
    grad_in_heads = scatter_grads(d_qkv, normed, [2 * DK + DV], "ctx")[0]
    grad_bias_here = jnp.sum(d_gate_in.astype(F32), axis=0)
    grad_rank_here = tn(rank_low, d_gate_in)
    d_rank_low = nt(d_gate_in, rank_out).astype(BF16)
    d_normed = nn(d_qkv, w_in_all) + nn(d_outgate, w_og_all) + nt(d_rank_low, rank_in)
    grad_rank_in_term = tn(normed, d_rank_low)
    grad_mixer_term = jnp.sum(d_normed * inputs * scale_one, axis=0)
    grad_in = reorder(d_resid + norm_back(d_normed, inputs, scale_one, gain_one), 1, True)[None]

    rank_out_here = jnp.take(grad_rank_here.reshape(RANK, heads, DK), head_order, axis=1)
    bias_here = jnp.take(grad_bias_here.reshape(heads, DK), head_order, axis=0)
    small = (
        reorder(grad_mixer_term, 0, True),
        reorder(grad_rank_in_term, 0, True),
        rank_out_here,
        bias_here,
        grad_group_term,
        reorder(grad_ffn_term, 0, True),
    )
    flat = sum_everywhere(jnp.concatenate([term.reshape(-1, DK) for term in small], axis=0))
    shared, at = [], 0
    for term in small:
        rows = term.size // DK
        shared.append(flat[at : at + rows])
        at += rows
    return (
        hidden_out,
        grad_in,
        shared[0].reshape(norm_mixer.shape),
        grad_in_heads[:DK].T,
        grad_in_heads[DK : 2 * DK].T,
        grad_in_heads[2 * DK :].T,
        grad_outgate.T,
        shared[1].reshape(w_rank_in.shape),
        shared[2].reshape(w_rank_out.shape),
        shared[3].reshape(gate_bias.shape),
        shared[4].reshape(group_gain.shape),
        grad_output,
        shared[5].reshape(norm_ffn.shape),
        grad_gate.T,
        grad_up.T,
        grad_down,
    )


def solution(mesh):
    sizes = dict(mesh.shape)
    cores = 2
    inner = Mesh(
        mesh.devices.reshape(sizes["dp"] // cores, cores, sizes["ctx"], sizes["tp"]),
        ("dpo", "core", "ctx", "tp"),
    )
    dp = ("dpo", "core")
    tokens = P(dp, ("ctx", "tp"), None)
    columns = P((*dp, "ctx"), "tp")
    rows = P("tp", (*dp, "ctx"))
    return jax.shard_map(
        on_device,
        mesh=inner,
        in_specs=(
            tokens,
            tokens,
            P(dp, None),
            P(),
            columns,
            columns,
            columns,
            columns,
            P(),
            P(),
            P(),
            P(),
            rows,
            P(),
            columns,
            columns,
            rows,
        ),
        out_specs=(
            tokens,
            tokens,
            P(),
            columns,
            columns,
            columns,
            columns,
            P(),
            P(),
            P(),
            P(),
            rows,
            P(),
            columns,
            columns,
            rows,
        ),
        check_vma=False,
    )
```

```python
import functools

import jax
import jax.numpy as jnp
from jax import lax
from jax.experimental import pallas as pl
from jax.experimental.pallas import tpu as pltpu
from jax.sharding import Mesh, PartitionSpec as P

DK = 128
DV = 256
RANK = 16
PIECE = 256
CHUNK = 128
EPSILON = 1e-06
GATE_NORM = 16.0
F32 = jnp.float32
BF16 = jnp.bfloat16
VMEM_LIMIT = 60 * 1024 * 1024


def nn(left, right):
    return lax.dot_general(left, right, (((1,), (0,)), ((), ())), preferred_element_type=F32)


def nt(left, right):
    return lax.dot_general(left, right, (((1,), (1,)), ((), ())), preferred_element_type=F32)


def tn(left, right):
    return lax.dot_general(left, right, (((0,), (0,)), ((), ())), preferred_element_type=F32)


def iota2(axis):
    return lax.broadcasted_iota(jnp.int32, (CHUNK, CHUNK), axis)


def split_dot(matrix, values, terms):
    total = None
    for _ in range(terms):
        part = values.astype(BF16)
        values = values - part.astype(F32)
        product = nn(matrix, part)
        total = product if total is None else total + product
    return total


def state_rows(state, log_decay):
    high = log_decay.astype(BF16).astype(F32)
    rows = lax.broadcasted_iota(jnp.int32, (16, DK), 0)
    extra = jnp.where(rows == 0, high, jnp.where(rows == 1, log_decay - high, 0.0))
    return jnp.concatenate([state, extra], axis=0).astype(BF16)


def states_kernel(chunks, qk_ref, value_ref, gate_ref, sums_ref, local_ref, future_ref, end_ref):
    lower = (iota2(0) >= iota2(1)).astype(BF16)
    state = jnp.zeros((DV, DK), F32)
    total = jnp.zeros((1, DK), F32)
    for j in range(chunks):
        rows = pl.ds(j * CHUNK, CHUNK)
        gate_in = gate_ref[rows, :]
        gate_log = (jnp.minimum(gate_in, 0.0) - jnp.log1p(jnp.exp(-jnp.abs(gate_in)))) * (
            1.0 / GATE_NORM
        )
        sums = split_dot(lower, gate_log, 3)
        sums_ref[rows, :] = sums
        last = sums[CHUNK - 1 : CHUNK, :]
        key_rows = qk_ref[rows, DK:].astype(F32)
        value_rows = value_ref[rows, :]
        local_ref[0, j] = state
        both = jnp.concatenate(
            [(key_rows * jnp.exp(last - sums)).astype(BF16), (key_rows * jnp.exp(sums)).astype(BF16)],
            axis=1,
        )
        update = tn(value_rows, both)
        state = state * jnp.exp(last) + update[:, :DK]
        total = total + last
        future_ref[0, j] = update[:, DK:].astype(BF16)
    end_ref[0] = state_rows(state, total)


def scores_of(queries, key_rows, sums, pic):
    middle = sums[CHUNK // 2 - 1 : CHUNK // 2, :]
    grow = jnp.exp(sums - middle)
    shrink = jnp.exp(middle - sums)
    q1 = (queries * grow).astype(BF16)
    k1 = (key_rows * shrink).astype(BF16)
    q2 = (queries * shrink).astype(BF16)
    k2 = (key_rows * grow).astype(BF16)
    row, col = iota2(0), iota2(1)
    diagonal = jnp.sum(queries * key_rows, axis=1, keepdims=True)
    above = jnp.logical_and(row < col, pic > 0)
    scores = jnp.where(
        row > col,
        nt(q1, k1),
        jnp.where(row == col, diagonal, jnp.where(above, nt(q2, k2), 0.0)),
    )
    return scores, q1, k1, q2, k2, grow, shrink, above


def mix_kernel(
    chunks,
    flags_ref,
    qk_ref,
    value_ref,
    sums_ref,
    local_ref,
    incoming_ref,
    future_ref,
    later_ref,
    outgate_ref,
    gain_ref,
    mixed_ref,
    gated_ref,
):
    incoming = incoming_ref[0].astype(F32)
    before = jnp.zeros((1, DK), F32)
    gain = gain_ref[...]
    for j in range(chunks):
        rows = pl.ds(j * CHUNK, CHUNK)
        sums = sums_ref[rows, :]
        last = sums[CHUNK - 1 : CHUNK, :]
        queries = qk_ref[rows, :DK].astype(F32) * DK**-0.5
        key_rows = qk_ref[rows, DK:].astype(F32)
        value_rows = value_ref[rows, :]
        scores = scores_of(queries, key_rows, sums, flags_ref[0, j])[0]
        state = (local_ref[0, j] + incoming * jnp.exp(before)).astype(BF16)
        later = later_ref[0] if j == chunks - 1 else future_ref[0, j + 1]
        cross = flags_ref[1, j].astype(F32)
        factors = jnp.concatenate(
            [
                (queries * jnp.exp(sums)).astype(BF16),
                (queries * (jnp.exp(last - sums) * cross)).astype(BF16),
            ],
            axis=1,
        )
        mixed = nn(scores.astype(BF16), value_rows) + nt(
            factors, jnp.concatenate([state, later], axis=1)
        )
        before = before + last
        mixed_ref[rows, :] = mixed
        scale = lax.rsqrt(jnp.mean(mixed * mixed, axis=1, keepdims=True) + EPSILON)
        gate = outgate_ref[rows, :]
        gated_ref[rows, :] = (mixed * scale * gain * gate * jax.nn.sigmoid(gate)).astype(BF16)


def gate_back_kernel(
    chunks,
    flags_ref,
    d_gated_ref,
    outgate_ref,
    mixed_ref,
    gain_ref,
    qk_ref,
    sums_ref,
    d_outgate_ref,
    d_mixed_ref,
    gain_grad_ref,
    local_ref,
    end_ref,
    earlier_ref,
):
    gain = gain_ref[...]
    state = jnp.zeros((DV, DK), F32)
    total = jnp.zeros((1, DK), F32)
    gain_grad = jnp.zeros((1, DV), F32)
    for j in reversed(range(chunks)):
        rows = pl.ds(j * CHUNK, CHUNK)
        d_gated = d_gated_ref[rows, :]
        gate = outgate_ref[rows, :]
        mixed = mixed_ref[rows, :]
        sigma = jax.nn.sigmoid(gate)
        scale = lax.rsqrt(jnp.mean(mixed * mixed, axis=1, keepdims=True) + EPSILON)
        unit = mixed * scale
        d_grouped = d_gated * gate * sigma
        slope = sigma * (1.0 + gate * (1.0 - sigma))
        d_outgate_ref[rows, :] = (d_gated * unit * gain * slope).astype(BF16)
        gain_grad = gain_grad + jnp.sum(d_grouped * unit, axis=0, keepdims=True)
        weighted = gain * d_grouped
        d_mixed = scale * (weighted - unit * jnp.mean(weighted * unit, axis=1, keepdims=True))
        d_low = d_mixed.astype(BF16)
        d_mixed_ref[rows, :] = d_low
        sums = sums_ref[rows, :]
        last = sums[CHUNK - 1 : CHUNK, :]
        queries = qk_ref[rows, :DK].astype(F32) * DK**-0.5
        local_ref[0, j] = state
        update = tn(d_low, (queries * jnp.exp(sums)).astype(BF16))
        if j == chunks - 1:
            cross = flags_ref[1, j].astype(F32)
            earlier_ref[0] = tn(
                d_low, (queries * (jnp.exp(last - sums) * cross)).astype(BF16)
            ).astype(BF16)
        state = state * jnp.exp(last) + update
        total = total + last
    gain_grad_ref[0] = gain_grad
    end_ref[0] = state_rows(state, total)


def mix_back_kernel(
    chunks,
    flags_ref,
    d_mixed_ref,
    qk_ref,
    value_ref,
    sums_ref,
    local_ref,
    incoming_ref,
    future_ref,
    later_ref,
    back_local_ref,
    back_incoming_ref,
    earlier_ref,
    gate_ref,
    d_qk_ref,
    d_value_ref,
    d_gate_ref,
):
    incoming = incoming_ref[0].astype(F32)
    back_incoming = back_incoming_ref[0].astype(F32)
    lasts = [sums_ref[pl.ds(j * CHUNK + CHUNK - 1, 1), :] for j in range(chunks)]
    row, col = iota2(0), iota2(1)
    upper = (row <= col).astype(BF16)
    before = jnp.zeros((1, DK), F32)
    d_future = earlier_ref[0]
    for j in range(chunks):
        rows = pl.ds(j * CHUNK, CHUNK)
        sums = sums_ref[rows, :]
        last = lasts[j]
        after = jnp.zeros((1, DK), F32)
        for l in range(j + 1, chunks):
            after = after + lasts[l]
        queries = qk_ref[rows, :DK].astype(F32) * DK**-0.5
        key_rows = qk_ref[rows, DK:].astype(F32)
        value_rows = value_ref[rows, :]
        d_mixed = d_mixed_ref[rows, :]
        scores, q1, k1, q2, k2, grow, shrink, above = scores_of(
            queries, key_rows, sums, flags_ref[0, j]
        )
        state = local_ref[0, j] + incoming * jnp.exp(before)
        back_state = back_local_ref[0, j] + back_incoming * jnp.exp(after)
        later = later_ref[0] if j == chunks - 1 else future_ref[0, j + 1]
        cross = flags_ref[1, j].astype(F32)
        from_start = jnp.exp(sums)
        to_end = jnp.exp(last - sums)
        to_later = to_end * cross
        d_scores = nt(d_mixed, value_rows)
        on_diagonal = jnp.sum(jnp.where(row == col, d_scores, 0.0), axis=1, keepdims=True)
        below = jnp.where(row > col, d_scores, 0.0).astype(BF16)
        ahead = jnp.where(above, d_scores, 0.0).astype(BF16)
        dq_causal = grow * nn(below, k1)
        dk_causal = shrink * tn(below, q1)
        dq_ahead = shrink * nn(ahead, k2)
        dk_ahead = grow * tn(ahead, q2)
        d_factors = nn(d_mixed, jnp.concatenate([state.astype(BF16), later], axis=1))
        dq_causal = dq_causal + from_start * d_factors[:, :DK]
        dq_later = to_later * d_factors[:, DK:]
        back_pair = jnp.concatenate([back_state.astype(BF16), d_future], axis=1)
        d_factors = nn(value_rows, back_pair)
        dk_state = to_end * d_factors[:, :DK]
        dk_earlier = from_start * d_factors[:, DK:]
        key_factors = jnp.concatenate(
            [(key_rows * to_end).astype(BF16), (key_rows * from_start).astype(BF16)], axis=1
        )
        d_values = tn(scores.astype(BF16), d_mixed) + nt(key_factors, back_pair)
        d_future = tn(d_mixed, (queries * to_later).astype(BF16)).astype(BF16)
        d_sums = queries * (dq_causal - dq_ahead - dq_later) + key_rows * (
            dk_ahead + dk_earlier - dk_causal - dk_state
        )
        d_last = (
            jnp.sum(key_rows * dk_state + queries * dq_later, axis=0, keepdims=True)
            + jnp.sum(state * back_state, axis=0, keepdims=True) * jnp.exp(last)
        )
        d_log = split_dot(upper, d_sums, 2) + d_last
        gate_in = gate_ref[rows, :]
        d_gate_ref[rows, :] = (d_log * jax.nn.sigmoid(-gate_in) * (1.0 / GATE_NORM)).astype(BF16)
        d_qk_ref[rows, :DK] = (
            (dq_causal + dq_ahead + dq_later + on_diagonal * key_rows) * DK**-0.5
        ).astype(BF16)
        d_qk_ref[rows, DK:] = (
            dk_causal + dk_ahead + dk_state + dk_earlier + on_diagonal * queries
        ).astype(BF16)
        d_value_ref[rows, :] = d_values.astype(BF16)
        before = before + last


def rows_block(length, width):
    return pl.BlockSpec((length, width), lambda h: (0, h))


def lead_block(*inner):
    return pl.BlockSpec((1, *inner), lambda h: (h,) + (0,) * len(inner))


def whole_block(*dims):
    return pl.BlockSpec(dims, lambda h: (0,) * len(dims))


def smem():
    return pl.BlockSpec(memory_space=pltpu.SMEM)


def params():
    return pltpu.CompilerParams(vmem_limit_bytes=VMEM_LIMIT)


def shaped(shape, kind):
    return jax.ShapeDtypeStruct(shape, kind)


def chunk_states(qk, values, gate_in, heads):
    length = qk.shape[0]
    chunks = length // CHUNK
    return pl.pallas_call(
        functools.partial(states_kernel, chunks),
        grid=(heads,),
        in_specs=[rows_block(length, 2 * DK), rows_block(length, DV), rows_block(length, DK)],
        out_specs=[
            rows_block(length, DK),
            lead_block(chunks, DV, DK),
            lead_block(chunks, DV, DK),
            lead_block(DV + 16, DK),
        ],
        out_shape=[
            shaped((length, heads * DK), F32),
            shaped((heads, chunks, DV, DK), F32),
            shaped((heads, chunks, DV, DK), BF16),
            shaped((heads, DV + 16, DK), BF16),
        ],
        compiler_params=params(),
        name="chunk_states",
    )(qk, values, gate_in)


def mix(flags, qk, values, sums, local, incoming, future, later, outgate, gain):
    length = qk.shape[0]
    heads, chunks = local.shape[:2]
    return pl.pallas_call(
        functools.partial(mix_kernel, chunks),
        grid=(heads,),
        in_specs=[
            smem(),
            rows_block(length, 2 * DK),
            rows_block(length, DV),
            rows_block(length, DK),
            lead_block(chunks, DV, DK),
            lead_block(DV, DK),
            lead_block(chunks, DV, DK),
            lead_block(DV, DK),
            rows_block(length, DV),
            whole_block(1, DV),
        ],
        out_specs=[rows_block(length, DV), rows_block(length, DV)],
        out_shape=[shaped((length, heads * DV), F32), shaped((length, heads * DV), BF16)],
        compiler_params=params(),
        name="mix",
    )(flags, qk, values, sums, local, incoming, future, later, outgate, gain)


def gate_back(flags, d_gated, outgate, mixed, gain, qk, sums, heads):
    length = qk.shape[0]
    chunks = length // CHUNK
    return pl.pallas_call(
        functools.partial(gate_back_kernel, chunks),
        grid=(heads,),
        in_specs=[
            smem(),
            rows_block(length, DV),
            rows_block(length, DV),
            rows_block(length, DV),
            whole_block(1, DV),
            rows_block(length, 2 * DK),
            rows_block(length, DK),
        ],
        out_specs=[
            rows_block(length, DV),
            rows_block(length, DV),
            lead_block(1, DV),
            lead_block(chunks, DV, DK),
            lead_block(DV + 16, DK),
            lead_block(DV, DK),
        ],
        out_shape=[
            shaped((length, heads * DV), BF16),
            shaped((length, heads * DV), BF16),
            shaped((heads, 1, DV), F32),
            shaped((heads, chunks, DV, DK), F32),
            shaped((heads, DV + 16, DK), BF16),
            shaped((heads, DV, DK), BF16),
        ],
        compiler_params=params(),
        name="gate_back",
    )(flags, d_gated, outgate, mixed, gain, qk, sums)


def mix_back(
    flags, d_mixed, qk, values, sums, local, incoming, future, later, back_local, back_incoming, earlier, gate_in
):
    length = qk.shape[0]
    heads, chunks = local.shape[:2]
    return pl.pallas_call(
        functools.partial(mix_back_kernel, chunks),
        grid=(heads,),
        in_specs=[
            smem(),
            rows_block(length, DV),
            rows_block(length, 2 * DK),
            rows_block(length, DV),
            rows_block(length, DK),
            lead_block(chunks, DV, DK),
            lead_block(DV, DK),
            lead_block(chunks, DV, DK),
            lead_block(DV, DK),
            lead_block(chunks, DV, DK),
            lead_block(DV, DK),
            lead_block(DV, DK),
            rows_block(length, DK),
        ],
        out_specs=[rows_block(length, 2 * DK), rows_block(length, DV), rows_block(length, DK)],
        out_shape=[
            shaped((length, heads * 2 * DK), BF16),
            shaped((length, heads * DV), BF16),
            shaped((length, heads * DK), BF16),
        ],
        compiler_params=params(),
        name="mix_back",
    )(
        flags, d_mixed, qk, values, sums, local, incoming, future, later, back_local, back_incoming, earlier, gate_in
    )


def chain_kernel(count, backwards, place_ref, *refs):
    parts, other_ref, total_ref = refs[:count], refs[count], refs[count + 1]
    outs, scratch, result = refs[count + 2 : 2 * count + 2], refs[-2], refs[-1]
    place, joined = place_ref[0], place_ref[1]
    for k in range(count):
        scratch[lax.rem(place + k, count)] = parts[k][...].astype(F32)
    state = jnp.where(joined > 0, other_ref[:DV, :].astype(F32), 0.0)
    for z in reversed(range(count)) if backwards else range(count):
        result[z] = state.astype(BF16)
        log_decay = scratch[z, DV : DV + 1, :] + scratch[z, DV + 1 : DV + 2, :]
        state = state * jnp.exp(log_decay) + scratch[z, :DV, :]
    total_ref[...] = state.astype(BF16)
    for k in range(count):
        outs[k][...] = result[lax.rem(place + k, count)]


def chain(parts, other, place, joined, backwards):
    count = len(parts)
    return pl.pallas_call(
        functools.partial(chain_kernel, count, backwards),
        in_specs=[smem()] + [pl.BlockSpec(memory_space=pltpu.VMEM)] * (count + 1),
        out_specs=[pl.BlockSpec(memory_space=pltpu.VMEM)] * (count + 1),
        out_shape=[shaped((DV, DK), BF16)] * (count + 1),
        scratch_shapes=[
            pltpu.VMEM((count, DV + 16, DK), F32),
            pltpu.VMEM((count, DV, DK), BF16),
        ],
        compiler_params=params(),
        name="chain",
    )(jnp.stack([place, joined]).astype(jnp.int32), *parts, other)


def shifted(array, axis, by):
    size = lax.axis_size(axis)
    return lax.ppermute(array, axis, [(i, (i + by) % size) for i in range(size)])


def swapped(array, axis):
    return lax.ppermute(array, axis, [(0, 1), (1, 0)])


def exchange_states(ends, backwards):
    count = lax.axis_size("tp")
    place = lax.axis_index("tp")
    side = lax.axis_index("ctx")
    parts = [ends[0]] + [shifted(ends[k], "tp", -k) for k in range(1, count)]
    zero = jnp.zeros((DV, DK), BF16)
    total = chain(parts, zero, place, jnp.zeros_like(place), backwards)[0]
    other = swapped(total, "ctx")
    joined = (side == 0) if backwards else (side == 1)
    outs = chain(parts, other, place, joined.astype(place.dtype), backwards)[1:]
    return jnp.stack([outs[0]] + [shifted(outs[k], "tp", k) for k in range(1, count)])


def neighbour_future(first, odd_to_even):
    size = lax.axis_size("tp")
    if odd_to_even:
        moved = lax.ppermute(first, "tp", [(i + 1, i) for i in range(0, size - 1, 2)])
        return jnp.concatenate([moved[1:], moved[:1]], axis=0)
    moved = lax.ppermute(first, "tp", [(i, i + 1) for i in range(0, size - 1, 2)])
    return jnp.concatenate([moved[-1:], moved[:-1]], axis=0)


def take_columns(ref, order_ref, out_ref):
    for j in range(8):
        out_ref[:, j * 128 : (j + 1) * 128] = ref[:, pl.ds(pl.multiple_of(order_ref[j] * 128, 128), 128)]


def begin_kernel(
    heads,
    order_ref,
    hidden_ref,
    cot_ref,
    gain_one_ref,
    gain_two_ref,
    rank_in_ref,
    rank_out_ref,
    bias_ref,
    inputs_ref,
    upstream_ref,
    normed_ref,
    new_one_ref,
    new_two_ref,
    new_rank_in_ref,
    new_rank_out_ref,
    new_bias_ref,
):
    take_columns(gain_one_ref, order_ref, new_one_ref)
    take_columns(gain_two_ref, order_ref, new_two_ref)
    for j in range(8):
        new_rank_in_ref[j * 128 : (j + 1) * 128, :] = rank_in_ref[
            pl.ds(pl.multiple_of(order_ref[j] * 128, 128), 128), :
        ]
    for k in range(heads):
        lanes = pl.ds(pl.multiple_of(order_ref[16 + k] * DK, DK), DK)
        new_rank_out_ref[:, k * DK : (k + 1) * DK] = rank_out_ref[:, lanes]
        new_bias_ref[:, k * DK : (k + 1) * DK] = bias_ref[:, lanes]
    take_columns(cot_ref, order_ref, upstream_ref)
    take_columns(hidden_ref, order_ref, inputs_ref)
    for i in range(hidden_ref.shape[0] // CHUNK):
        rows = pl.ds(i * CHUNK, CHUNK)
        values = inputs_ref[rows, :].astype(F32)
        scale = lax.rsqrt(jnp.mean(values * values, axis=1, keepdims=True) + EPSILON)
        normed_ref[rows, :] = (values * scale * new_one_ref[...]).astype(BF16)


def call_whole(kernel, smem_args, args, outs, name):
    vmem = pl.BlockSpec(memory_space=pltpu.VMEM)
    return pl.pallas_call(
        kernel,
        in_specs=[smem()] * len(smem_args) + [vmem] * len(args),
        out_specs=[vmem] * len(outs),
        out_shape=outs,
        compiler_params=params(),
        name=name,
    )(*smem_args, *args)


def output_kernel(back_ref, resid_ref, feed_ref, out_ref):
    for j in range(8):
        lanes = pl.ds(pl.multiple_of(back_ref[8 + j] * 128, 128), 128)
        out_ref[:, j * 128 : (j + 1) * 128] = (resid_ref[:, lanes] + feed_ref[:, lanes]).astype(BF16)


def finish_kernel(heads, back_ref, d_resid_ref, d_normed_ref, inputs_ref, gain_ref, rank_in_ref, rank_out_ref,
                  bias_ref, group_ref, ffn_ref, grad_ref, small_ref, scratch):
    gain = gain_ref[...]
    total = jnp.zeros((1, gain.shape[1]), F32)
    for i in range(inputs_ref.shape[0] // CHUNK):
        rows = pl.ds(i * CHUNK, CHUNK)
        values = inputs_ref[rows, :].astype(F32)
        scale = lax.rsqrt(jnp.mean(values * values, axis=1, keepdims=True) + EPSILON)
        unit = values * scale
        upstream = d_normed_ref[rows, :]
        total = total + jnp.sum(upstream * unit, axis=0, keepdims=True)
        weighted = upstream * gain
        scratch[0:CHUNK, :] = d_resid_ref[rows, :] + scale * (
            weighted - unit * jnp.mean(weighted * unit, axis=1, keepdims=True)
        )
        for j in range(8):
            lanes = pl.ds(pl.multiple_of(back_ref[8 + j] * 128, 128), 128)
            grad_ref[rows, j * 128 : (j + 1) * 128] = scratch[0:CHUNK, lanes]
    small_ref[...] = jnp.zeros_like(small_ref)
    scratch[0:16, :] = rank_in_ref[...]
    scratch[24:25, :] = total
    scratch[25:26, :] = ffn_ref[...]
    for j in range(8):
        lanes = pl.ds(pl.multiple_of(back_ref[8 + j] * 128, 128), 128)
        small_ref[0:16, j * 128 : (j + 1) * 128] = scratch[0:16, lanes]
        small_ref[24:26, j * 128 : (j + 1) * 128] = scratch[24:26, lanes]
    width = heads * DK
    for k in range(heads):
        lanes = pl.ds(pl.multiple_of(back_ref[16 + k] * DK, DK), DK)
        small_ref[16:24, k * DK : (k + 1) * DK] = rank_out_ref[0:8, lanes]
        small_ref[16:24, width + k * DK : width + (k + 1) * DK] = rank_out_ref[8:16, lanes]
        small_ref[26:27, k * DK : (k + 1) * DK] = bias_ref[:, lanes]
    small_ref[26:27, width : width + DV] = group_ref[...]


def split_axes():
    return all(lax.axis_size(axis) == 2 for axis in ("dpo", "core", "ctx"))


def column_order():
    heads = lax.axis_size("tp")
    place = lax.axis_index("tp")
    order, back = list(range(8)), list(range(8))
    if split_axes():
        y, core, x = (lax.axis_index(axis) for axis in ("dpo", "core", "ctx"))
        for j in range(8):
            high, middle, last = j >> 2, (j >> 1) & 1, j & 1
            order[j] = ((y ^ middle) * 2 + (core ^ high)) * 2 + (x ^ last)
            back[j] = ((core ^ middle) * 2 + (y ^ high)) * 2 + (x ^ last)
    slots = [lax.rem(place - k + heads, heads) for k in range(heads)]
    return jnp.stack([jnp.asarray(v, jnp.int32) for v in order + back + slots])


def tie(array, *others):
    others = [other for other in others if other is not None]
    return lax.optimization_barrier((array, *others))[0] if others else array


def weight_axes(first):
    return ("ctx", "dpo") if first == "ctx" else ("dpo", "ctx")


def join_kernel(swap, *refs):
    out = refs[-1]
    for i in range(4):
        for half in range(2):
            block = 4 * (i // 2) + (2 * half + i % 2 if swap else 2 * (i % 2) + half)
            out[:, block * 128 : (block + 1) * 128] = refs[2 * i + half][...]


def join_columns(pieces, swap):
    rows = pieces[0].shape[0] // 2
    tile = 512
    specs, args = [], []
    for piece in pieces:
        for half in range(2):
            specs.append(pl.BlockSpec((tile, 128), functools.partial(lambda at, i: (at + i, 0), half * (rows // tile))))
            args.append(piece)
    return pl.pallas_call(
        functools.partial(join_kernel, swap),
        grid=(rows // tile,),
        in_specs=specs,
        out_specs=pl.BlockSpec((tile, 1024), lambda i: (i, 0)),
        out_shape=shaped((rows, 1024), pieces[0].dtype),
        compiler_params=params(),
        name="join",
    )(*args)


def ffn_kernel(
    units,
    order_ref,
    every_ref,
    rows_ref,
    upstream_ref,
    feed_ref,
    d_rows_ref,
    grads_ref,
    near_ref,
    far_ref,
    weights,
    lefts,
):
    rows, upstream = rows_ref[...], upstream_ref[...]
    for j in range(8):
        weights[:, j * 128 : (j + 1) * 128] = every_ref[order_ref[j], 0]
    both, down = weights[: 2 * units, :], weights[2 * units :, :]
    gate_pre = nt(weights[:units, :], rows)
    sigma = jax.nn.sigmoid(gate_pre)
    silu = gate_pre * sigma
    slope = sigma * (1.0 + gate_pre * (1.0 - sigma))
    up_pre = nt(weights[units : 2 * units, :], rows)
    d_act = nt(down, upstream)
    lefts[2 * units :, :] = (silu * up_pre).astype(BF16)
    lefts[:units, :] = (d_act * up_pre * slope).astype(BF16)
    lefts[units : 2 * units, :] = (d_act * silu).astype(BF16)
    d_rows = tn(lefts[: 2 * units, :], both)
    feed = tn(lefts[2 * units :, :], down)

    @pl.when(pl.program_id(0) == 0)
    def _():
        d_rows_ref[...] = d_rows
        feed_ref[...] = feed

    @pl.when(pl.program_id(0) > 0)
    def _():
        d_rows_ref[...] += d_rows
        feed_ref[...] += feed

    for pair in range(4):
        lanes = slice(pair * 256, (pair + 1) * 256)
        grads_in = nn(lefts[: 2 * units, :], rows[:, lanes]).astype(BF16)
        grads_down = nn(lefts[2 * units :, :], upstream[:, lanes]).astype(BF16)
        down_ref = near_ref if pair < 2 else far_ref
        for j in range(2):
            block = order_ref[2 * pair + j]
            grads_ref[block, 0, : 2 * units, :] = grads_in[:, j * 128 : (j + 1) * 128]
            down_ref[2 * (pair % 2) + j, 0] = grads_down[:, j * 128 : (j + 1) * 128]
    padding = grads_ref.shape[2] - 2 * units
    if padding:
        grads_ref[:, 0, 2 * units :, :] = jnp.zeros((8, padding, 128), BF16)


def feed_forward(order, every, rows, upstream):
    length, width = rows.shape
    blocks, slots, total, _ = every.shape
    units = total // 3
    padded = -(-2 * units // 48) * 48
    whole = pl.BlockSpec((length, width), lambda t, order: (0, 0))
    half = pl.BlockSpec((4, 1, units, 128), lambda t, order: (0, t, 0, 0))
    return pl.pallas_call(
        functools.partial(ffn_kernel, units),
        grid_spec=pltpu.PrefetchScalarGridSpec(
            num_scalar_prefetch=1,
            grid=(slots,),
            in_specs=[
                pl.BlockSpec((blocks, 1, total, 128), lambda t, order: (0, t, 0, 0)),
                whole,
                whole,
            ],
            out_specs=[
                whole,
                whole,
                pl.BlockSpec((blocks, 1, padded, 128), lambda t, order: (0, t, 0, 0)),
                half,
                half,
            ],
            scratch_shapes=[pltpu.VMEM((total, width), BF16), pltpu.VMEM((total, length), BF16)],
        ),
        out_shape=[
            shaped((length, width), F32),
            shaped((length, width), F32),
            shaped((blocks, slots, padded, 128), BF16),
            shaped((4, slots, units, 128), BF16),
            shaped((4, slots, units, 128), BF16),
        ],
        compiler_params=params(),
        name="feed_forward",
    )(order, every, rows, upstream)


def gather_units(parts):
    count = lax.axis_size("tp")
    shard = jnp.concatenate(parts, axis=0)
    rows = shard.shape[0]
    if not split_axes():
        wide = lax.all_gather(shard, ("dpo", "core", "ctx"), axis=1, tiled=True)
        every = lax.all_gather(wide, "tp").reshape(count, rows, 8, 128)
        return jnp.transpose(every, (2, 0, 1, 3))
    every = lax.all_gather(shard, ("dpo", "core", "ctx", "tp"))
    return every.reshape(8, count, rows, 128)


def scatter_units(grads):
    blocks, count, rows, lanes = grads.shape
    if not split_axes():
        whole = jnp.transpose(grads, (1, 2, 0, 3)).reshape(count, rows, blocks * lanes)
        whole = lax.psum_scatter(whole, "tp", scatter_dimension=0, tiled=True)[0]
        return lax.psum_scatter(whole, ("dpo", "core", "ctx"), scatter_dimension=1, tiled=True)
    return lax.psum_scatter(
        grads.reshape(blocks * count, rows, lanes), ("dpo", "core", "ctx", "tp"), scatter_dimension=0
    )


def gather_slots(shards):
    count = lax.axis_size("tp")
    shard = jnp.concatenate(shards, axis=0)
    slots = [shard] + [shifted(shard, "tp", k) for k in range(1, count)]
    stacks, at = [], 0
    for part in shards:
        stacks.append([slot[at : at + part.shape[0]] for slot in slots])
        at += part.shape[0]
    return stacks


class Gather:
    def __init__(self, stacks, first):
        self.first = weight_axes(first)
        self.stack = jnp.concatenate(sum(stacks, []), axis=0)

    def hop_one(self, *hold):
        own = tie(self.stack, *hold)
        if not split_axes():
            self.whole = lax.all_gather(own, ("dpo", "core", "ctx"), axis=1, tiled=True)
            return None
        self.own = own
        self.near = swapped(own, self.first[0])
        return self.near

    def hop_two(self, *hold):
        if not split_axes():
            return None
        self.pair = tie(jnp.concatenate([self.own, self.near], axis=0), *hold)
        self.far = swapped(self.pair, self.first[1])
        return self.far

    def hop_core(self, *hold):
        if not split_axes():
            return self.whole
        far = tie(self.far, *hold)
        pieces = [self.pair, far, swapped(self.pair, "core"), swapped(far, "core")]
        return join_columns(pieces, self.first[0] == "dpo")


class Scatter:
    def __init__(self, first):
        self.first = weight_axes(first)

    def core(self, far):
        self.sent = far
        if split_axes():
            self.received = swapped(far, "core")
        return far

    def one(self, near):
        if not split_axes():
            self.kept = jnp.concatenate([near, self.sent.astype(F32)], axis=-1)
            return None
        near = near + self.received.astype(F32)
        quarter = near.shape[-1] // 4
        blocks = [near[..., i * quarter : (i + 1) * quarter] for i in range(4)]
        if self.first[0] == "ctx":
            kept, sent = (blocks[0], blocks[2]), (blocks[1], blocks[3])
        else:
            kept, sent = (blocks[0], blocks[1]), (blocks[2], blocks[3])
        self.kept = jnp.concatenate(kept, axis=-1).astype(BF16)
        self.sent = jnp.concatenate(sent, axis=-1).astype(BF16)
        self.received = swapped(self.sent, self.first[0])
        return self.sent

    def two(self, *hold):
        if not split_axes():
            return None
        kept = tie(self.kept, *hold)
        quarter = kept.shape[-1] // 2
        sums = kept.astype(F32) + self.received.astype(F32)
        self.kept, self.sent = sums[..., :quarter].astype(BF16), sums[..., quarter:].astype(BF16)
        self.received = swapped(self.sent, self.first[1])
        return self.sent

    def sums(self, *hold):
        kept = tie(self.kept, *hold)
        if not split_axes():
            return kept
        return (kept.astype(F32) + self.received.astype(F32)).astype(BF16)


class BlockScatter(Scatter):
    def one(self, near, received):
        total = near.astype(F32) + received.astype(F32)
        one, two = ((0, 2), (1, 3)) if self.first[0] == "ctx" else ((0, 1), (2, 3))
        self.kept = jnp.stack([total[i] for i in one]).astype(BF16)
        self.sent = jnp.stack([total[i] for i in two]).astype(BF16)
        self.received = swapped(self.sent, self.first[0])
        return self.sent

    def two(self, *hold):
        kept = tie(self.kept, *hold)
        self.kept, self.sent = (
            (kept[i].astype(F32) + self.received[i].astype(F32)).astype(BF16) for i in range(2)
        )
        self.received = swapped(self.sent, self.first[1])
        return self.sent


def hop_two_together(ones, *hold):
    if not split_axes():
        return None
    kept, sent = [], []
    for one in ones:
        quarter = one.kept.shape[-1] // 2
        sums = tie(one.kept, *hold).astype(F32) + one.received.astype(F32)
        kept.append(sums[..., :quarter].astype(BF16))
        sent.append(sums[..., quarter:].astype(BF16))
    received = swapped(jnp.concatenate(sent, axis=0), ones[0].first[1])
    at = 0
    for i, one in enumerate(ones):
        rows = kept[i].shape[0]
        one.kept, one.received = kept[i], received[at : at + rows]
        at += rows
    return received


def send_slots(slots):
    count = lax.axis_size("tp")
    return [slots[0]] + [shifted(slots[k], "tp", -k) for k in range(1, count)]


def add_slots(parts):
    total = parts[0].astype(F32)
    for part in parts[1:]:
        total = total + part.astype(F32)
    if not split_axes():
        total = lax.psum_scatter(
            total, ("dpo", "core", "ctx"), scatter_dimension=total.ndim - 1, tiled=True
        )
    return total


def ordered_sum_kernel(count, order_ref, *refs):
    scratch, out_ref = refs[-1], refs[-2]
    for k in range(count):
        scratch[k] = refs[k][...].astype(F32)
    total = scratch[order_ref[16]]
    for z in range(1, count):
        total = total + scratch[order_ref[16 + z]]
    out_ref[...] = total


def sum_here(values):
    for axis in ("core", "ctx", "dpo"):
        values = values + swapped(values, axis)
    return values


def sum_slots(parts, order):
    vmem = pl.BlockSpec(memory_space=pltpu.VMEM)
    shape = parts[0].shape
    return pl.pallas_call(
        functools.partial(ordered_sum_kernel, len(parts)),
        in_specs=[smem()] + [vmem] * len(parts),
        out_specs=vmem,
        out_shape=shaped(shape, F32),
        scratch_shapes=[pltpu.VMEM((len(parts), *shape), F32)],
        compiler_params=params(),
        name="ordered_sum",
    )(order, *parts)


def rms_scale(values):
    return lax.rsqrt(jnp.mean(values * values, axis=-1, keepdims=True) + EPSILON)


def norm_back(upstream, values, scale, gain):
    weighted = upstream * gain
    return scale * weighted - values * scale**3 * jnp.mean(
        weighted * values, axis=-1, keepdims=True
    )


def on_device(
    hidden_in,
    cotangent,
    pic_starts,
    norm_mixer,
    w_query,
    w_key,
    w_value,
    w_outgate,
    w_rank_in,
    w_rank_out,
    gate_bias,
    group_gain,
    w_output,
    norm_ffn,
    w_gate,
    w_up,
    w_down,
):
    seq_count, length, width = hidden_in.shape
    assert seq_count == 1 and width == 1024 and length % CHUNK == 0
    heads = lax.axis_size("tp")
    place = lax.axis_index("tp")
    chunks = length // CHUNK
    units = w_down.shape[0]

    stacks = gather_slots(
        [jnp.concatenate([w_query.T, w_key.T], axis=0), w_outgate.T, w_value.T, w_output]
    )
    takes = [Gather(stacks[:2], "dpo"), Gather(stacks[2:], "ctx")]
    order = column_order()
    ffn_all = gather_units([w_gate.T, w_up.T, w_down])
    first_hops = [take.hop_one() for take in takes]
    for take in takes:
        take.hop_two(*first_hops)
    w_one, w_two = (take.hop_core() for take in takes)
    w_qk, w_og_all = w_one[: heads * 2 * DK], w_one[heads * 2 * DK :]
    w_val, w_out_all = w_two[: heads * DV], w_two[heads * DV :]

    kinds = [
        shaped((length, width), BF16),
        shaped((length, width), BF16),
        shaped((length, width), BF16),
        shaped((1, width), F32),
        shaped((1, width), F32),
        shaped((width, RANK), BF16),
        shaped((RANK, heads * DK), BF16),
        shaped((1, heads * DK), F32),
    ]
    inputs_low, upstream, normed, gain_one, gain_two, rank_in, rank_out, bias = call_whole(
        functools.partial(begin_kernel, heads),
        [order],
        [
            hidden_in[0],
            cotangent[0],
            norm_mixer.astype(F32)[None],
            norm_ffn.astype(F32)[None],
            w_rank_in,
            w_rank_out,
            gate_bias.astype(F32)[None],
        ],
        kinds,
        "begin",
    )
    inputs = inputs_low.astype(F32)

    part = lax.axis_index("ctx") * heads + place
    starts = part * length + jnp.arange(chunks, dtype=jnp.int32) * CHUNK
    inside = (starts[:, None] >= pic_starts[0][None, :]) & (
        starts[:, None] < pic_starts[0][None, :] + PIECE
    )
    in_piece = jnp.any(inside, axis=1)
    first_half = (starts % PIECE) == 0
    flags = jnp.stack([in_piece, in_piece & first_half]).astype(jnp.int32)

    rank_low = nn(normed, rank_in).astype(BF16)
    gate_in = nn(rank_low, rank_out) + bias
    qk = nt(normed, w_qk).astype(BF16)
    values = nt(normed, w_val).astype(BF16)
    sums, local, future, ends = chunk_states(qk, values, gate_in, heads)
    later = neighbour_future(future[:, 0], True)
    incoming = exchange_states(ends, False)
    outgate = nt(normed, w_og_all)
    gain_group = group_gain.astype(F32)[None, :]
    mixed, gated = mix(flags, qk, values, sums, local, incoming, future, later, outgate, gain_group)
    resid = inputs + nn(gated, w_out_all)
    scale_two = rms_scale(resid)
    normed_two = (resid * scale_two * gain_two).astype(BF16)

    side = width // 2
    feed, d_norm_two, grads_ffn, near_down, far_down = feed_forward(
        order, ffn_all, normed_two, upstream
    )
    grads_ffn = scatter_units(grads_ffn)
    fast = split_axes()
    pairs = heads // 2
    give_down = [BlockScatter("ctx"), BlockScatter("dpo")]
    received_down = swapped(far_down, "core") if fast else None

    def step_down(step, *args):
        return [getattr(one, step)(*args) for one in give_down] if fast else []

    grad_ffn_term = jnp.sum(d_norm_two * resid * scale_two, axis=0, keepdims=True)
    d_resid = upstream.astype(F32) + norm_back(d_norm_two, resid, scale_two, gain_two)
    d_branch = d_resid.astype(BF16)
    give_out, give_gate = Scatter("ctx"), Scatter("dpo")
    d_gated = nt(d_branch, w_out_all)
    if fast:
        sent_down = [
            give_down[i].one(
                near_down[:, i * pairs : (i + 1) * pairs], received_down[:, i * pairs : (i + 1) * pairs]
            )
            for i in range(2)
        ]
        d_gated = tie(d_gated, *sent_down)
    d_outgate, d_mixed, gain_terms, back_local, back_ends, earlier = gate_back(
        flags, d_gated, outgate, mixed, gain_group, qk, sums, heads
    )
    grad_group_term = jnp.sum(gain_terms, axis=0)
    earlier = neighbour_future(earlier, False)
    back_incoming = exchange_states(back_ends, True)
    give_out.core(tn(gated, d_branch[:, side:]).astype(BF16))
    give_gate.core(tn(d_outgate, normed[:, side:]).astype(BF16))
    near_out = give_out.one(tn(gated, d_branch[:, :side]))
    near_gate = give_gate.one(tn(d_outgate, normed[:, :side]))
    d_mixed = tie(d_mixed, near_out, near_gate)
    d_qk, d_val, d_gate_in = mix_back(
        flags, d_mixed, qk, values, sums, local, incoming, future, later, back_local, back_incoming, earlier, gate_in
    )
    give_qk, give_val = Scatter("dpo"), Scatter("ctx")
    far_in = [
        give_qk.core(tn(d_qk, normed[:, side:]).astype(BF16)),
        give_val.core(tn(d_val, normed[:, side:]).astype(BF16)),
    ]
    second_down = step_down("two", *far_in)
    grad_bias_here = jnp.sum(d_gate_in.astype(F32), axis=0, keepdims=True)
    grad_rank_here = tn(rank_low, d_gate_in)
    d_rank_low = nt(d_gate_in, rank_out).astype(BF16)
    d_low = tie(d_qk, *far_in, *second_down)
    d_normed = nn(d_low, w_qk) + nn(d_val, w_val) + nn(d_outgate, w_og_all) + nt(d_rank_low, rank_in)
    d_tied = tie((d_qk, d_val), d_normed)
    near_in = [give_qk.one(tn(d_tied[0], normed[:, :side])), give_val.one(tn(d_tied[1], normed[:, :side]))]
    d_normed = tie(d_normed, *near_in)
    grad_rank_in_term = tn(d_rank_low, normed)
    grad_in, small = pl.pallas_call(
        functools.partial(finish_kernel, heads),
        in_specs=[smem()] + [pl.BlockSpec(memory_space=pltpu.VMEM)] * 9,
        out_specs=[pl.BlockSpec(memory_space=pltpu.VMEM)] * 2,
        out_shape=[shaped((length, width), F32), shaped((32, width), F32)],
        scratch_shapes=[pltpu.VMEM((CHUNK, width), F32)],
        compiler_params=params(),
        name="finish",
    )(
        order,
        d_resid,
        d_normed,
        inputs_low,
        gain_one,
        grad_rank_in_term,
        grad_rank_here,
        grad_bias_here,
        grad_group_term,
        grad_ffn_term,
    )
    sums_down = step_down("sums", *near_in)
    if fast:
        slots_down = jnp.concatenate(sums_down, axis=0)
        parts_down = lax.all_to_all(slots_down, "tp", 0, 0, tiled=True)
        grad_down = add_slots([parts_down[k] for k in range(heads)])
    else:
        slots_down = jnp.concatenate([near_down, far_down], axis=0)
        slots_down = jnp.transpose(slots_down, (1, 2, 0, 3)).reshape(heads, units, width)
        grad_down = lax.psum_scatter(slots_down.astype(F32), "tp", scatter_dimension=0, tiled=True)
        grad_down = add_slots([grad_down[0]])
    hop_two_together([give_out, give_val])
    hop_two_together([give_gate, give_qk])
    slots_in = [
        one.sums().reshape(heads, DV, -1) for one in (give_out, give_gate, give_qk, give_val)
    ]
    slots_in = [[part[k] for part in slots_in] for k in range(heads)]
    if fast:
        small = sum_here(small).astype(BF16)
        parts_in = send_slots(
            [jnp.concatenate(slot + [small.reshape(-1, DK)], axis=0) for slot in slots_in]
        )
        rows = parts_in[0].shape[0] - small.size // DK
        small = sum_slots([part[rows:].reshape(small.shape) for part in parts_in], order)
        mixer_grads = add_slots([part[:rows] for part in parts_in])
    else:
        small = lax.psum(small, ("dpo", "core", "ctx", "tp"))
        mixer_grads = add_slots(send_slots([jnp.concatenate(slot, axis=0) for slot in slots_in]))
    hidden_out = call_whole(
        output_kernel, [order], [resid, feed], [shaped((length, width), BF16)], "output"
    )[0][None]
    grad_output, grad_outgate, grad_heads = mixer_grads[:DV], mixer_grads[DV : 2 * DV], mixer_grads[2 * DV :]
    grads_ffn = grads_ffn.astype(F32)
    grad_gate, grad_up = grads_ffn[:units], grads_ffn[units : 2 * units]
    return (
        hidden_out,
        grad_in[None],
        small[24],
        grad_heads[:DK].T,
        grad_heads[DK : 2 * DK].T,
        grad_heads[2 * DK :].T,
        grad_outgate.T,
        small[:RANK].T,
        jnp.concatenate([small[16:24, : heads * DK], small[16:24, heads * DK :]], axis=0),
        small[26, : heads * DK],
        small[26, heads * DK : heads * DK + DV],
        grad_output,
        small[25],
        grad_gate.T,
        grad_up.T,
        grad_down,
    )


def solution(mesh):
    sizes = dict(mesh.shape)
    cores = 2
    inner = Mesh(
        mesh.devices.reshape(sizes["dp"] // cores, cores, sizes["ctx"], sizes["tp"]),
        ("dpo", "core", "ctx", "tp"),
    )
    dp = ("dpo", "core")
    tokens = P(dp, ("ctx", "tp"), None)
    columns = P((*dp, "ctx"), "tp")
    rows = P("tp", (*dp, "ctx"))
    return jax.shard_map(
        on_device,
        mesh=inner,
        in_specs=(
            tokens,
            tokens,
            P(dp, None),
            P(),
            columns,
            columns,
            columns,
            columns,
            P(),
            P(),
            P(),
            P(),
            rows,
            P(),
            columns,
            columns,
            rows,
        ),
        out_specs=(
            tokens,
            tokens,
            P(),
            columns,
            columns,
            columns,
            columns,
            P(),
            P(),
            P(),
            P(),
            rows,
            P(),
            columns,
            columns,
            rows,
        ),
        check_vma=False,
    )
```

```python
import functools

import jax
import jax.numpy as jnp
from jax import lax
from jax.experimental import pallas as pl
from jax.experimental.pallas import tpu as pltpu
from jax.sharding import Mesh, PartitionSpec as P

DK = 128
DV = 256
RANK = 16
PIECE = 256
CHUNK = 128
EPSILON = 1e-06
GATE_NORM = 16.0
F32 = jnp.float32
BF16 = jnp.bfloat16
VMEM_LIMIT = 60 * 1024 * 1024


def nn(left, right):
    return lax.dot_general(left, right, (((1,), (0,)), ((), ())), preferred_element_type=F32)


def nt(left, right):
    return lax.dot_general(left, right, (((1,), (1,)), ((), ())), preferred_element_type=F32)


def tn(left, right):
    return lax.dot_general(left, right, (((0,), (0,)), ((), ())), preferred_element_type=F32)


def iota2(axis):
    return lax.broadcasted_iota(jnp.int32, (CHUNK, CHUNK), axis)


def split_dot(matrix, values, terms):
    total = None
    for _ in range(terms):
        part = values.astype(BF16)
        values = values - part.astype(F32)
        product = nn(matrix, part)
        total = product if total is None else total + product
    return total


def state_rows(state, log_decay):
    high = log_decay.astype(BF16).astype(F32)
    rows = lax.broadcasted_iota(jnp.int32, (16, DK), 0)
    extra = jnp.where(rows == 0, high, jnp.where(rows == 1, log_decay - high, 0.0))
    return jnp.concatenate([state, extra], axis=0).astype(BF16)


def states_kernel(chunks, qk_ref, value_ref, gate_ref, sums_ref, local_ref, future_ref, end_ref):
    lower = (iota2(0) >= iota2(1)).astype(BF16)
    state = jnp.zeros((DV, DK), F32)
    total = jnp.zeros((1, DK), F32)
    for j in range(chunks):
        rows = pl.ds(j * CHUNK, CHUNK)
        gate_in = gate_ref[rows, :]
        gate_log = (jnp.minimum(gate_in, 0.0) - jnp.log1p(jnp.exp(-jnp.abs(gate_in)))) * (
            1.0 / GATE_NORM
        )
        sums = split_dot(lower, gate_log, 3)
        sums_ref[rows, :] = sums
        last = sums[CHUNK - 1 : CHUNK, :]
        key_rows = qk_ref[rows, DK:].astype(F32)
        value_rows = value_ref[rows, :]
        local_ref[0, j] = state
        both = jnp.concatenate(
            [(key_rows * jnp.exp(last - sums)).astype(BF16), (key_rows * jnp.exp(sums)).astype(BF16)],
            axis=1,
        )
        update = tn(value_rows, both)
        state = state * jnp.exp(last) + update[:, :DK]
        total = total + last
        future_ref[0, j] = update[:, DK:].astype(BF16)
    end_ref[0] = state_rows(state, total)


def scores_of(queries, key_rows, sums, pic):
    middle = sums[CHUNK // 2 - 1 : CHUNK // 2, :]
    grow = jnp.exp(sums - middle)
    shrink = jnp.exp(middle - sums)
    q1 = (queries * grow).astype(BF16)
    k1 = (key_rows * shrink).astype(BF16)
    q2 = (queries * shrink).astype(BF16)
    k2 = (key_rows * grow).astype(BF16)
    row, col = iota2(0), iota2(1)
    diagonal = jnp.sum(queries * key_rows, axis=1, keepdims=True)
    above = jnp.logical_and(row < col, pic > 0)
    scores = jnp.where(
        row > col,
        nt(q1, k1),
        jnp.where(row == col, diagonal, jnp.where(above, nt(q2, k2), 0.0)),
    )
    return scores, q1, k1, q2, k2, grow, shrink, above


def mix_kernel(
    chunks,
    flags_ref,
    qk_ref,
    value_ref,
    sums_ref,
    local_ref,
    incoming_ref,
    future_ref,
    later_ref,
    outgate_ref,
    gain_ref,
    mixed_ref,
    gated_ref,
):
    incoming = incoming_ref[0].astype(F32)
    before = jnp.zeros((1, DK), F32)
    gain = gain_ref[...]
    for j in range(chunks):
        rows = pl.ds(j * CHUNK, CHUNK)
        sums = sums_ref[rows, :]
        last = sums[CHUNK - 1 : CHUNK, :]
        queries = qk_ref[rows, :DK].astype(F32) * DK**-0.5
        key_rows = qk_ref[rows, DK:].astype(F32)
        value_rows = value_ref[rows, :]
        scores = scores_of(queries, key_rows, sums, flags_ref[0, j])[0]
        state = (local_ref[0, j] + incoming * jnp.exp(before)).astype(BF16)
        later = later_ref[0] if j == chunks - 1 else future_ref[0, j + 1]
        cross = flags_ref[1, j].astype(F32)
        factors = jnp.concatenate(
            [
                (queries * jnp.exp(sums)).astype(BF16),
                (queries * (jnp.exp(last - sums) * cross)).astype(BF16),
            ],
            axis=1,
        )
        mixed = nn(scores.astype(BF16), value_rows) + nt(
            factors, jnp.concatenate([state, later], axis=1)
        )
        before = before + last
        mixed_ref[rows, :] = mixed
        scale = lax.rsqrt(jnp.mean(mixed * mixed, axis=1, keepdims=True) + EPSILON)
        gate = outgate_ref[rows, :]
        gated_ref[rows, :] = (mixed * scale * gain * gate * jax.nn.sigmoid(gate)).astype(BF16)


def gate_back_kernel(
    chunks,
    flags_ref,
    d_gated_ref,
    outgate_ref,
    mixed_ref,
    gain_ref,
    qk_ref,
    sums_ref,
    d_outgate_ref,
    d_mixed_ref,
    gain_grad_ref,
    local_ref,
    end_ref,
    earlier_ref,
):
    gain = gain_ref[...]
    state = jnp.zeros((DV, DK), F32)
    total = jnp.zeros((1, DK), F32)
    gain_grad = jnp.zeros((1, DV), F32)
    for j in reversed(range(chunks)):
        rows = pl.ds(j * CHUNK, CHUNK)
        d_gated = d_gated_ref[rows, :]
        gate = outgate_ref[rows, :]
        mixed = mixed_ref[rows, :]
        sigma = jax.nn.sigmoid(gate)
        scale = lax.rsqrt(jnp.mean(mixed * mixed, axis=1, keepdims=True) + EPSILON)
        unit = mixed * scale
        d_grouped = d_gated * gate * sigma
        slope = sigma * (1.0 + gate * (1.0 - sigma))
        d_outgate_ref[rows, :] = (d_gated * unit * gain * slope).astype(BF16)
        gain_grad = gain_grad + jnp.sum(d_grouped * unit, axis=0, keepdims=True)
        weighted = gain * d_grouped
        d_mixed = scale * (weighted - unit * jnp.mean(weighted * unit, axis=1, keepdims=True))
        d_low = d_mixed.astype(BF16)
        d_mixed_ref[rows, :] = d_low
        sums = sums_ref[rows, :]
        last = sums[CHUNK - 1 : CHUNK, :]
        queries = qk_ref[rows, :DK].astype(F32) * DK**-0.5
        local_ref[0, j] = state
        update = tn(d_low, (queries * jnp.exp(sums)).astype(BF16))
        if j == chunks - 1:
            cross = flags_ref[1, j].astype(F32)
            earlier_ref[0] = tn(
                d_low, (queries * (jnp.exp(last - sums) * cross)).astype(BF16)
            ).astype(BF16)
        state = state * jnp.exp(last) + update
        total = total + last
    gain_grad_ref[0] = gain_grad
    end_ref[0] = state_rows(state, total)


def mix_back_kernel(
    chunks,
    flags_ref,
    d_mixed_ref,
    qk_ref,
    value_ref,
    sums_ref,
    local_ref,
    incoming_ref,
    future_ref,
    later_ref,
    back_local_ref,
    back_incoming_ref,
    earlier_ref,
    gate_ref,
    d_qk_ref,
    d_value_ref,
    d_gate_ref,
):
    incoming = incoming_ref[0].astype(F32)
    back_incoming = back_incoming_ref[0].astype(F32)
    lasts = [sums_ref[pl.ds(j * CHUNK + CHUNK - 1, 1), :] for j in range(chunks)]
    row, col = iota2(0), iota2(1)
    upper = (row <= col).astype(BF16)
    before = jnp.zeros((1, DK), F32)
    d_future = earlier_ref[0]
    for j in range(chunks):
        rows = pl.ds(j * CHUNK, CHUNK)
        sums = sums_ref[rows, :]
        last = lasts[j]
        after = jnp.zeros((1, DK), F32)
        for l in range(j + 1, chunks):
            after = after + lasts[l]
        queries = qk_ref[rows, :DK].astype(F32) * DK**-0.5
        key_rows = qk_ref[rows, DK:].astype(F32)
        value_rows = value_ref[rows, :]
        d_mixed = d_mixed_ref[rows, :]
        scores, q1, k1, q2, k2, grow, shrink, above = scores_of(
            queries, key_rows, sums, flags_ref[0, j]
        )
        state = local_ref[0, j] + incoming * jnp.exp(before)
        back_state = back_local_ref[0, j] + back_incoming * jnp.exp(after)
        later = later_ref[0] if j == chunks - 1 else future_ref[0, j + 1]
        cross = flags_ref[1, j].astype(F32)
        from_start = jnp.exp(sums)
        to_end = jnp.exp(last - sums)
        to_later = to_end * cross
        d_scores = nt(d_mixed, value_rows)
        on_diagonal = jnp.sum(jnp.where(row == col, d_scores, 0.0), axis=1, keepdims=True)
        below = jnp.where(row > col, d_scores, 0.0).astype(BF16)
        ahead = jnp.where(above, d_scores, 0.0).astype(BF16)
        dq_causal = grow * nn(below, k1)
        dk_causal = shrink * tn(below, q1)
        dq_ahead = shrink * nn(ahead, k2)
        dk_ahead = grow * tn(ahead, q2)
        d_factors = nn(d_mixed, jnp.concatenate([state.astype(BF16), later], axis=1))
        dq_causal = dq_causal + from_start * d_factors[:, :DK]
        dq_later = to_later * d_factors[:, DK:]
        back_pair = jnp.concatenate([back_state.astype(BF16), d_future], axis=1)
        d_factors = nn(value_rows, back_pair)
        dk_state = to_end * d_factors[:, :DK]
        dk_earlier = from_start * d_factors[:, DK:]
        key_factors = jnp.concatenate(
            [(key_rows * to_end).astype(BF16), (key_rows * from_start).astype(BF16)], axis=1
        )
        d_values = tn(scores.astype(BF16), d_mixed) + nt(key_factors, back_pair)
        d_future = tn(d_mixed, (queries * to_later).astype(BF16)).astype(BF16)
        d_sums = queries * (dq_causal - dq_ahead - dq_later) + key_rows * (
            dk_ahead + dk_earlier - dk_causal - dk_state
        )
        d_last = (
            jnp.sum(key_rows * dk_state + queries * dq_later, axis=0, keepdims=True)
            + jnp.sum(state * back_state, axis=0, keepdims=True) * jnp.exp(last)
        )
        d_log = split_dot(upper, d_sums, 2) + d_last
        gate_in = gate_ref[rows, :]
        d_gate_ref[rows, :] = (d_log * jax.nn.sigmoid(-gate_in) * (1.0 / GATE_NORM)).astype(BF16)
        d_qk_ref[rows, :DK] = (
            (dq_causal + dq_ahead + dq_later + on_diagonal * key_rows) * DK**-0.5
        ).astype(BF16)
        d_qk_ref[rows, DK:] = (
            dk_causal + dk_ahead + dk_state + dk_earlier + on_diagonal * queries
        ).astype(BF16)
        d_value_ref[rows, :] = d_values.astype(BF16)
        before = before + last


def rows_block(length, width):
    return pl.BlockSpec((length, width), lambda h: (0, h))


def lead_block(*inner):
    return pl.BlockSpec((1, *inner), lambda h: (h,) + (0,) * len(inner))


def whole_block(*dims):
    return pl.BlockSpec(dims, lambda h: (0,) * len(dims))


def smem():
    return pl.BlockSpec(memory_space=pltpu.SMEM)


def params():
    return pltpu.CompilerParams(vmem_limit_bytes=VMEM_LIMIT)


def shaped(shape, kind):
    return jax.ShapeDtypeStruct(shape, kind)


def chunk_states(qk, values, gate_in, heads):
    length = qk.shape[0]
    chunks = length // CHUNK
    return pl.pallas_call(
        functools.partial(states_kernel, chunks),
        grid=(heads,),
        in_specs=[rows_block(length, 2 * DK), rows_block(length, DV), rows_block(length, DK)],
        out_specs=[
            rows_block(length, DK),
            lead_block(chunks, DV, DK),
            lead_block(chunks, DV, DK),
            lead_block(DV + 16, DK),
        ],
        out_shape=[
            shaped((length, heads * DK), F32),
            shaped((heads, chunks, DV, DK), F32),
            shaped((heads, chunks, DV, DK), BF16),
            shaped((heads, DV + 16, DK), BF16),
        ],
        compiler_params=params(),
        name="chunk_states",
    )(qk, values, gate_in)


def mix(flags, qk, values, sums, local, incoming, future, later, outgate, gain):
    length = qk.shape[0]
    heads, chunks = local.shape[:2]
    return pl.pallas_call(
        functools.partial(mix_kernel, chunks),
        grid=(heads,),
        in_specs=[
            smem(),
            rows_block(length, 2 * DK),
            rows_block(length, DV),
            rows_block(length, DK),
            lead_block(chunks, DV, DK),
            lead_block(DV, DK),
            lead_block(chunks, DV, DK),
            lead_block(DV, DK),
            rows_block(length, DV),
            whole_block(1, DV),
        ],
        out_specs=[rows_block(length, DV), rows_block(length, DV)],
        out_shape=[shaped((length, heads * DV), F32), shaped((length, heads * DV), BF16)],
        compiler_params=params(),
        name="mix",
    )(flags, qk, values, sums, local, incoming, future, later, outgate, gain)


def gate_back(flags, d_gated, outgate, mixed, gain, qk, sums, heads):
    length = qk.shape[0]
    chunks = length // CHUNK
    return pl.pallas_call(
        functools.partial(gate_back_kernel, chunks),
        grid=(heads,),
        in_specs=[
            smem(),
            rows_block(length, DV),
            rows_block(length, DV),
            rows_block(length, DV),
            whole_block(1, DV),
            rows_block(length, 2 * DK),
            rows_block(length, DK),
        ],
        out_specs=[
            rows_block(length, DV),
            rows_block(length, DV),
            lead_block(1, DV),
            lead_block(chunks, DV, DK),
            lead_block(DV + 16, DK),
            lead_block(DV, DK),
        ],
        out_shape=[
            shaped((length, heads * DV), BF16),
            shaped((length, heads * DV), BF16),
            shaped((heads, 1, DV), F32),
            shaped((heads, chunks, DV, DK), F32),
            shaped((heads, DV + 16, DK), BF16),
            shaped((heads, DV, DK), BF16),
        ],
        compiler_params=params(),
        name="gate_back",
    )(flags, d_gated, outgate, mixed, gain, qk, sums)


def mix_back(
    flags, d_mixed, qk, values, sums, local, incoming, future, later, back_local, back_incoming, earlier, gate_in
):
    length = qk.shape[0]
    heads, chunks = local.shape[:2]
    return pl.pallas_call(
        functools.partial(mix_back_kernel, chunks),
        grid=(heads,),
        in_specs=[
            smem(),
            rows_block(length, DV),
            rows_block(length, 2 * DK),
            rows_block(length, DV),
            rows_block(length, DK),
            lead_block(chunks, DV, DK),
            lead_block(DV, DK),
            lead_block(chunks, DV, DK),
            lead_block(DV, DK),
            lead_block(chunks, DV, DK),
            lead_block(DV, DK),
            lead_block(DV, DK),
            rows_block(length, DK),
        ],
        out_specs=[rows_block(length, 2 * DK), rows_block(length, DV), rows_block(length, DK)],
        out_shape=[
            shaped((length, heads * 2 * DK), BF16),
            shaped((length, heads * DV), BF16),
            shaped((length, heads * DK), BF16),
        ],
        compiler_params=params(),
        name="mix_back",
    )(
        flags, d_mixed, qk, values, sums, local, incoming, future, later, back_local, back_incoming, earlier, gate_in
    )


def chain_kernel(count, backwards, place_ref, *refs):
    parts, other_ref, total_ref = refs[:count], refs[count], refs[count + 1]
    outs, scratch, result = refs[count + 2 : 2 * count + 2], refs[-2], refs[-1]
    place, joined = place_ref[0], place_ref[1]
    for k in range(count):
        scratch[lax.rem(place + k, count)] = parts[k][...].astype(F32)
    state = jnp.where(joined > 0, other_ref[:DV, :].astype(F32), 0.0)
    for z in reversed(range(count)) if backwards else range(count):
        result[z] = state.astype(BF16)
        log_decay = scratch[z, DV : DV + 1, :] + scratch[z, DV + 1 : DV + 2, :]
        state = state * jnp.exp(log_decay) + scratch[z, :DV, :]
    total_ref[...] = state.astype(BF16)
    for k in range(count):
        outs[k][...] = result[lax.rem(place + k, count)]


def chain(parts, other, place, joined, backwards):
    count = len(parts)
    return pl.pallas_call(
        functools.partial(chain_kernel, count, backwards),
        in_specs=[smem()] + [pl.BlockSpec(memory_space=pltpu.VMEM)] * (count + 1),
        out_specs=[pl.BlockSpec(memory_space=pltpu.VMEM)] * (count + 1),
        out_shape=[shaped((DV, DK), BF16)] * (count + 1),
        scratch_shapes=[
            pltpu.VMEM((count, DV + 16, DK), F32),
            pltpu.VMEM((count, DV, DK), BF16),
        ],
        compiler_params=params(),
        name="chain",
    )(jnp.stack([place, joined]).astype(jnp.int32), *parts, other)


def shifted(array, axis, by):
    size = lax.axis_size(axis)
    return lax.ppermute(array, axis, [(i, (i + by) % size) for i in range(size)])


def swapped(array, axis):
    return lax.ppermute(array, axis, [(0, 1), (1, 0)])


def exchange_states(ends, backwards):
    count = lax.axis_size("tp")
    place = lax.axis_index("tp")
    side = lax.axis_index("ctx")
    parts = [ends[0]] + [shifted(ends[k], "tp", -k) for k in range(1, count)]
    zero = jnp.zeros((DV, DK), BF16)
    total = chain(parts, zero, place, jnp.zeros_like(place), backwards)[0]
    other = swapped(total, "ctx")
    joined = (side == 0) if backwards else (side == 1)
    outs = chain(parts, other, place, joined.astype(place.dtype), backwards)[1:]
    return jnp.stack([outs[0]] + [shifted(outs[k], "tp", k) for k in range(1, count)])


def neighbour_future(first, odd_to_even):
    size = lax.axis_size("tp")
    if odd_to_even:
        moved = lax.ppermute(first, "tp", [(i + 1, i) for i in range(0, size - 1, 2)])
        return jnp.concatenate([moved[1:], moved[:1]], axis=0)
    moved = lax.ppermute(first, "tp", [(i, i + 1) for i in range(0, size - 1, 2)])
    return jnp.concatenate([moved[-1:], moved[:-1]], axis=0)


def take_columns(ref, order_ref, out_ref):
    for j in range(8):
        out_ref[:, j * 128 : (j + 1) * 128] = ref[:, pl.ds(pl.multiple_of(order_ref[j] * 128, 128), 128)]


def begin_kernel(
    heads,
    order_ref,
    hidden_ref,
    cot_ref,
    gain_one_ref,
    gain_two_ref,
    rank_in_ref,
    rank_out_ref,
    bias_ref,
    inputs_ref,
    upstream_ref,
    normed_ref,
    new_one_ref,
    new_two_ref,
    new_rank_in_ref,
    new_rank_out_ref,
    new_bias_ref,
):
    take_columns(gain_one_ref, order_ref, new_one_ref)
    take_columns(gain_two_ref, order_ref, new_two_ref)
    take_columns(rank_in_ref, order_ref, new_rank_in_ref)
    for k in range(heads):
        lanes = pl.ds(pl.multiple_of(order_ref[16 + k] * DK, DK), DK)
        new_rank_out_ref[:, k * DK : (k + 1) * DK] = rank_out_ref[:, lanes]
        new_bias_ref[:, k * DK : (k + 1) * DK] = bias_ref[:, lanes]
    take_columns(cot_ref, order_ref, upstream_ref)
    take_columns(hidden_ref, order_ref, inputs_ref)
    for i in range(hidden_ref.shape[0] // CHUNK):
        rows = pl.ds(i * CHUNK, CHUNK)
        values = inputs_ref[rows, :].astype(F32)
        scale = lax.rsqrt(jnp.mean(values * values, axis=1, keepdims=True) + EPSILON)
        normed_ref[rows, :] = (values * scale * new_one_ref[...]).astype(BF16)


def call_whole(kernel, smem_args, args, outs, name):
    vmem = pl.BlockSpec(memory_space=pltpu.VMEM)
    return pl.pallas_call(
        kernel,
        in_specs=[smem()] * len(smem_args) + [vmem] * len(args),
        out_specs=[vmem] * len(outs),
        out_shape=outs,
        compiler_params=params(),
        name=name,
    )(*smem_args, *args)


def pack_kernel(q_ref, k_ref, v_ref, g_ref, o_ref, gate_ref, up_ref, down_ref, mixer_ref, ffn_ref):
    at = 0
    for ref in (q_ref, k_ref, g_ref, v_ref):
        for i in range(ref.shape[1] // 128):
            mixer_ref[at : at + 128, :] = ref[:, i * 128 : (i + 1) * 128].T
            at += 128
    mixer_ref[at:, :] = o_ref[...]
    units = down_ref.shape[0]
    for i, ref in enumerate((gate_ref, up_ref)):
        ffn_ref[i * units : (i + 1) * units, :] = ref[...]
    ffn_ref[2 * units :, :] = down_ref[...]


def pack_weights(w_query, w_key, w_value, w_outgate, w_output, w_gate, w_up, w_down):
    if not split_axes():
        mixer = [w_query.T, w_key.T, w_outgate.T, w_value.T, w_output]
        return jnp.concatenate(mixer, axis=0), jnp.concatenate([w_gate.T, w_up.T, w_down], axis=0)
    args = (w_query, w_key, w_value, w_outgate, w_output, w_gate.T, w_up.T, w_down)
    rows = 2 * DK + 3 * DV
    return call_whole(
        pack_kernel,
        [],
        args,
        [shaped((rows, 128), BF16), shaped((3 * w_down.shape[0], 128), BF16)],
        "pack",
    )


def output_kernel(back_ref, resid_ref, feed_ref, out_ref):
    for j in range(8):
        lanes = pl.ds(pl.multiple_of(back_ref[8 + j] * 128, 128), 128)
        out_ref[:, j * 128 : (j + 1) * 128] = (resid_ref[:, lanes] + feed_ref[:, lanes]).astype(BF16)


def finish_kernel(heads, back_ref, d_resid_ref, d_normed_ref, inputs_ref, gain_ref, rank_in_ref, rank_out_ref,
                  bias_ref, group_ref, ffn_ref, grad_ref, small_ref, scratch):
    gain = gain_ref[...]
    total = jnp.zeros((1, gain.shape[1]), F32)
    for i in range(inputs_ref.shape[0] // CHUNK):
        rows = pl.ds(i * CHUNK, CHUNK)
        values = inputs_ref[rows, :].astype(F32)
        scale = lax.rsqrt(jnp.mean(values * values, axis=1, keepdims=True) + EPSILON)
        unit = values * scale
        upstream = d_normed_ref[rows, :]
        total = total + jnp.sum(upstream * unit, axis=0, keepdims=True)
        weighted = upstream * gain
        scratch[0:CHUNK, :] = d_resid_ref[rows, :] + scale * (
            weighted - unit * jnp.mean(weighted * unit, axis=1, keepdims=True)
        )
        for j in range(8):
            lanes = pl.ds(pl.multiple_of(back_ref[8 + j] * 128, 128), 128)
            grad_ref[rows, j * 128 : (j + 1) * 128] = scratch[0:CHUNK, lanes]
    small_ref[...] = jnp.zeros_like(small_ref)
    scratch[0:16, :] = rank_in_ref[...]
    scratch[24:25, :] = total
    scratch[25:26, :] = ffn_ref[...]
    for j in range(8):
        lanes = pl.ds(pl.multiple_of(back_ref[8 + j] * 128, 128), 128)
        small_ref[j * 32 : j * 32 + 16, :] = scratch[0:16, lanes]
        small_ref[j * 32 + 24 : j * 32 + 26, :] = scratch[24:26, lanes]
    for k in range(heads):
        lanes = pl.ds(pl.multiple_of(back_ref[16 + k] * DK, DK), DK)
        small_ref[k * 32 + 16 : k * 32 + 24, :] = rank_out_ref[0:8, lanes]
        small_ref[(heads + k) * 32 + 16 : (heads + k) * 32 + 24, :] = rank_out_ref[8:16, lanes]
        small_ref[k * 32 + 26 : k * 32 + 27, :] = bias_ref[:, lanes]
    for k in range(DV // 128):
        small_ref[(heads + k) * 32 + 26 : (heads + k) * 32 + 27, :] = group_ref[:, k * 128 : (k + 1) * 128]


def last_kernel(heads, count, order_ref, *refs):
    parts, outs, scratch = refs[:count], refs[count:-1], refs[-1]
    q_ref, k_ref, v_ref, g_ref, o_ref, mixer_ref, in_ref, out_ref, bias_ref, group_ref, ffn_ref = outs
    small = 4 * DV

    def summed(at, rows):
        total = parts[0][at : at + rows, :].astype(F32)
        for part in parts[1:]:
            total = total + part[at : at + rows, :].astype(F32)
        return total

    o_ref[...] = summed(0, DV)
    at = DV
    for ref in (g_ref, q_ref, k_ref, v_ref):
        for i in range(ref.shape[1] // 128):
            ref[:, i * 128 : (i + 1) * 128] = summed(at, 128).T
            at += 128
    for k in range(count):
        scratch[k] = parts[k][small:, :].astype(F32)
    total = scratch[order_ref[16]]
    for z in range(1, count):
        total = total + scratch[order_ref[16 + z]]
    for j in range(8):
        lanes = slice(j * 128, (j + 1) * 128)
        block = total[j * 32 : (j + 1) * 32]
        in_ref[:, lanes] = block[0:16]
        mixer_ref[:, lanes] = block[24:25]
        ffn_ref[:, lanes] = block[25:26]
        k = j % heads
        out_ref[(j // heads) * 8 : (j // heads) * 8 + 8, k * DK : (k + 1) * DK] = block[16:24]
        if j < heads:
            bias_ref[:, lanes] = block[26:27]
        elif j < heads + DV // 128:
            group_ref[:, k * 128 : (k + 1) * 128] = block[26:27]


def split_axes():
    return all(lax.axis_size(axis) == 2 for axis in ("dpo", "core", "ctx"))


def column_order():
    heads = lax.axis_size("tp")
    place = lax.axis_index("tp")
    order, back = list(range(8)), list(range(8))
    if split_axes():
        y, core, x = (lax.axis_index(axis) for axis in ("dpo", "core", "ctx"))
        for j in range(8):
            high, middle, last = j >> 2, (j >> 1) & 1, j & 1
            order[j] = ((y ^ middle) * 2 + (core ^ high)) * 2 + (x ^ last)
            back[j] = ((core ^ middle) * 2 + (y ^ high)) * 2 + (x ^ last)
    slots = [lax.rem(place - k + heads, heads) for k in range(heads)]
    return jnp.stack([jnp.asarray(v, jnp.int32) for v in order + back + slots])


def tie(array, *others):
    others = [other for other in others if other is not None]
    return lax.optimization_barrier((array, *others))[0] if others else array


def weight_axes(first):
    return ("ctx", "dpo") if first == "ctx" else ("dpo", "ctx")


def join_kernel(swap, *refs):
    out = refs[-1]
    for i in range(4):
        for half in range(2):
            block = 4 * (i // 2) + (2 * half + i % 2 if swap else 2 * (i % 2) + half)
            out[:, block * 128 : (block + 1) * 128] = refs[2 * i + half][...]


def join_columns(pieces, swap, part):
    rows = pieces[0].shape[0] // 4
    tile = 512
    specs, args = [], []
    for piece in pieces:
        for half in range(2):
            start = (2 * half + part) * (rows // tile)
            specs.append(pl.BlockSpec((tile, 128), functools.partial(lambda at, i: (at + i, 0), start)))
            args.append(piece)
    return pl.pallas_call(
        functools.partial(join_kernel, swap),
        grid=(rows // tile,),
        in_specs=specs,
        out_specs=pl.BlockSpec((tile, 1024), lambda i: (i, 0)),
        out_shape=shaped((rows, 1024), pieces[0].dtype),
        compiler_params=params(),
        name="join",
    )(*args)


def ffn_kernel(
    units,
    order_ref,
    every_ref,
    rows_ref,
    upstream_ref,
    feed_ref,
    d_rows_ref,
    grads_ref,
    near_ref,
    far_ref,
    weights,
    lefts,
):
    rows, upstream = rows_ref[...], upstream_ref[...]
    for j in range(8):
        weights[:, j * 128 : (j + 1) * 128] = every_ref[order_ref[j], 0]
    both, down = weights[: 2 * units, :], weights[2 * units :, :]
    gate_pre = nt(weights[:units, :], rows)
    sigma = jax.nn.sigmoid(gate_pre)
    silu = gate_pre * sigma
    slope = sigma * (1.0 + gate_pre * (1.0 - sigma))
    up_pre = nt(weights[units : 2 * units, :], rows)
    d_act = nt(down, upstream)
    lefts[2 * units :, :] = (silu * up_pre).astype(BF16)
    lefts[:units, :] = (d_act * up_pre * slope).astype(BF16)
    lefts[units : 2 * units, :] = (d_act * silu).astype(BF16)
    d_rows = tn(lefts[: 2 * units, :], both)
    feed = tn(lefts[2 * units :, :], down)

    @pl.when(pl.program_id(0) == 0)
    def _():
        d_rows_ref[...] = d_rows
        feed_ref[...] = feed

    @pl.when(pl.program_id(0) > 0)
    def _():
        d_rows_ref[...] += d_rows
        feed_ref[...] += feed

    for pair in range(4):
        lanes = slice(pair * 256, (pair + 1) * 256)
        grads_in = nn(lefts[: 2 * units, :], rows[:, lanes]).astype(BF16)
        grads_down = nn(lefts[2 * units :, :], upstream[:, lanes]).astype(BF16)
        down_ref = near_ref if pair < 2 else far_ref
        for j in range(2):
            block = order_ref[2 * pair + j]
            grads_ref[block, 0, : 2 * units, :] = grads_in[:, j * 128 : (j + 1) * 128]
            down_ref[2 * (pair % 2) + j, 0] = grads_down[:, j * 128 : (j + 1) * 128]
    padding = grads_ref.shape[2] - 2 * units
    if padding:
        grads_ref[:, 0, 2 * units :, :] = jnp.zeros((8, padding, 128), BF16)


def feed_forward(order, every, rows, upstream):
    length, width = rows.shape
    blocks, slots, total, _ = every.shape
    units = total // 3
    padded = -(-2 * units // 48) * 48
    whole = pl.BlockSpec((length, width), lambda t, order: (0, 0))
    half = pl.BlockSpec((4, 1, units, 128), lambda t, order: (0, t, 0, 0))
    return pl.pallas_call(
        functools.partial(ffn_kernel, units),
        grid_spec=pltpu.PrefetchScalarGridSpec(
            num_scalar_prefetch=1,
            grid=(slots,),
            in_specs=[
                pl.BlockSpec((blocks, 1, total, 128), lambda t, order: (0, t, 0, 0)),
                whole,
                whole,
            ],
            out_specs=[
                whole,
                whole,
                pl.BlockSpec((blocks, 1, padded, 128), lambda t, order: (0, t, 0, 0)),
                half,
                half,
            ],
            scratch_shapes=[pltpu.VMEM((total, width), BF16), pltpu.VMEM((total, length), BF16)],
        ),
        out_shape=[
            shaped((length, width), F32),
            shaped((length, width), F32),
            shaped((blocks, slots, padded, 128), BF16),
            shaped((4, slots, units, 128), BF16),
            shaped((4, slots, units, 128), BF16),
        ],
        compiler_params=params(),
        name="feed_forward",
    )(order, every, rows, upstream)


def gather_units(shard):
    count = lax.axis_size("tp")
    rows = shard.shape[0]
    if not split_axes():
        wide = lax.all_gather(shard, ("dpo", "core", "ctx"), axis=1, tiled=True)
        every = lax.all_gather(wide, "tp").reshape(count, rows, 8, 128)
        return jnp.transpose(every, (2, 0, 1, 3))
    every = lax.all_gather(shard, ("dpo", "core", "ctx", "tp"))
    return every.reshape(8, count, rows, 128)


def scatter_units(grads):
    blocks, count, rows, lanes = grads.shape
    if not split_axes():
        whole = jnp.transpose(grads, (1, 2, 0, 3)).reshape(count, rows, blocks * lanes)
        whole = lax.psum_scatter(whole, "tp", scatter_dimension=0, tiled=True)[0]
        return lax.psum_scatter(whole, ("dpo", "core", "ctx"), scatter_dimension=1, tiled=True)
    return lax.psum_scatter(
        grads.reshape(blocks * count, rows, lanes), ("dpo", "core", "ctx", "tp"), scatter_dimension=0
    )


def gather_slots(shard, sizes):
    count = lax.axis_size("tp")
    slots = [shard] + [shifted(shard, "tp", k) for k in range(1, count)]
    stacks, at = [], 0
    for size in sizes:
        stacks.append([slot[at : at + size] for slot in slots])
        at += size
    return stacks


class Gather:
    def __init__(self, stacks, first):
        self.first = weight_axes(first)
        self.stack = jnp.concatenate(sum(stacks, []), axis=0)

    def hop_one(self, *hold):
        own = tie(self.stack, *hold)
        if not split_axes():
            self.whole = lax.all_gather(own, ("dpo", "core", "ctx"), axis=1, tiled=True)
            return None
        self.own = own
        self.near = swapped(own, self.first[0])
        return self.near

    def hop_two(self, *hold):
        if not split_axes():
            return None
        self.pair = tie(jnp.concatenate([self.own, self.near], axis=0), *hold)
        self.far = swapped(self.pair, self.first[1])
        return self.far

    def hop_core(self):
        if split_axes():
            self.pieces = [
                self.pair, self.far, swapped(self.pair, "core"), swapped(self.far, "core")
            ]

    def join(self, part, *hold):
        if not split_axes():
            rows = self.whole.shape[0] // 2
            return self.whole[part * rows : (part + 1) * rows]
        pieces = [tie(self.pieces[0], *hold)] + self.pieces[1:]
        return join_columns(pieces, self.first[0] == "dpo", part)


class Scatter:
    def __init__(self, first):
        self.first = weight_axes(first)

    def core(self, far):
        self.sent = far
        if split_axes():
            self.received = swapped(far, "core")
        return far

    def one(self, nears):
        if not split_axes():
            near = jnp.concatenate(nears, axis=0)
            self.kept = jnp.concatenate([near, self.sent.astype(F32)], axis=-1)
            return None
        kept, sent, at = [], [], 0
        for near in nears:
            near = near + self.received[at : at + near.shape[0]].astype(F32)
            at += near.shape[0]
            quarter = near.shape[-1] // 4
            blocks = [near[:, i * quarter : (i + 1) * quarter] for i in range(4)]
            if self.first[0] == "ctx":
                mine, other = (blocks[0], blocks[2]), (blocks[1], blocks[3])
            else:
                mine, other = (blocks[0], blocks[1]), (blocks[2], blocks[3])
            kept.append(jnp.concatenate(mine, axis=-1).astype(BF16))
            sent.append(jnp.concatenate(other, axis=-1).astype(BF16))
        self.kept, self.sent = jnp.concatenate(kept, axis=0), jnp.concatenate(sent, axis=0)
        self.received = swapped(self.sent, self.first[0])
        return self.sent

    def two(self, *hold):
        if not split_axes():
            return None
        kept = tie(self.kept, *hold)
        quarter = kept.shape[-1] // 2
        sums = kept.astype(F32) + self.received.astype(F32)
        self.kept, self.sent = sums[..., :quarter].astype(BF16), sums[..., quarter:].astype(BF16)
        self.received = swapped(self.sent, self.first[1])
        return self.sent

    def sums(self, *hold):
        kept = tie(self.kept, *hold)
        if not split_axes():
            return kept
        return (kept.astype(F32) + self.received.astype(F32)).astype(BF16)


class BlockScatter(Scatter):
    def one(self, near, received):
        total = near.astype(F32) + received.astype(F32)
        one, two = ((0, 2), (1, 3)) if self.first[0] == "ctx" else ((0, 1), (2, 3))
        self.kept = jnp.stack([total[i] for i in one]).astype(BF16)
        self.sent = jnp.stack([total[i] for i in two]).astype(BF16)
        self.received = swapped(self.sent, self.first[0])
        return self.sent

    def two(self, *hold):
        kept = tie(self.kept, *hold)
        self.kept, self.sent = (
            (kept[i].astype(F32) + self.received[i].astype(F32)).astype(BF16) for i in range(2)
        )
        self.received = swapped(self.sent, self.first[1])
        return self.sent


def send_slots(slots):
    count = lax.axis_size("tp")
    return [slots[0]] + [shifted(slots[k], "tp", -k) for k in range(1, count)]


def add_slots(parts):
    total = parts[0].astype(F32)
    for part in parts[1:]:
        total = total + part.astype(F32)
    if not split_axes():
        total = lax.psum_scatter(
            total, ("dpo", "core", "ctx"), scatter_dimension=total.ndim - 1, tiled=True
        )
    return total


def sum_here(values):
    for axis in ("core", "ctx", "dpo"):
        values = values + swapped(values, axis)
    return values


def rms_scale(values):
    return lax.rsqrt(jnp.mean(values * values, axis=-1, keepdims=True) + EPSILON)


def norm_back(upstream, values, scale, gain):
    weighted = upstream * gain
    return scale * weighted - values * scale**3 * jnp.mean(
        weighted * values, axis=-1, keepdims=True
    )


def on_device(
    hidden_in,
    cotangent,
    pic_starts,
    norm_mixer,
    w_query,
    w_key,
    w_value,
    w_outgate,
    w_rank_in,
    w_rank_out,
    gate_bias,
    group_gain,
    w_output,
    norm_ffn,
    w_gate,
    w_up,
    w_down,
):
    seq_count, length, width = hidden_in.shape
    assert seq_count == 1 and width == 1024 and length % CHUNK == 0
    heads = lax.axis_size("tp")
    place = lax.axis_index("tp")
    chunks = length // CHUNK
    units = w_down.shape[0]

    mixer_shard, ffn_shard = pack_weights(
        w_query, w_key, w_value, w_outgate, w_output, w_gate, w_up, w_down
    )
    stacks = gather_slots(mixer_shard, [2 * DK, DV, DV, DV])
    takes = [Gather(stacks[:2], "dpo"), Gather(stacks[2:], "ctx")]
    order = column_order()
    ffn_all = gather_units(ffn_shard)
    kinds = [
        shaped((length, width), BF16),
        shaped((length, width), BF16),
        shaped((length, width), BF16),
        shaped((1, width), F32),
        shaped((1, width), F32),
        shaped((RANK, width), BF16),
        shaped((RANK, heads * DK), BF16),
        shaped((1, heads * DK), F32),
    ]
    inputs_low, upstream, normed, gain_one, gain_two, rank_in, rank_out, bias = call_whole(
        functools.partial(begin_kernel, heads),
        [order],
        [
            hidden_in[0],
            cotangent[0],
            norm_mixer.astype(F32)[None],
            norm_ffn.astype(F32)[None],
            w_rank_in.T,
            w_rank_out,
            gate_bias.astype(F32)[None],
        ],
        kinds,
        "begin",
    )
    inputs = inputs_low.astype(F32)

    part = lax.axis_index("ctx") * heads + place
    starts = part * length + jnp.arange(chunks, dtype=jnp.int32) * CHUNK
    inside = (starts[:, None] >= pic_starts[0][None, :]) & (
        starts[:, None] < pic_starts[0][None, :] + PIECE
    )
    in_piece = jnp.any(inside, axis=1)
    first_half = (starts % PIECE) == 0
    flags = jnp.stack([in_piece, in_piece & first_half]).astype(jnp.int32)

    rank_low = nt(normed, rank_in).astype(BF16)
    gate_in = nn(rank_low, rank_out) + bias
    first_hops = [take.hop_one() for take in takes]
    for take in takes:
        take.hop_two(*first_hops, gate_in)
    for take in takes:
        take.hop_core()
    w_qk, w_val = (take.join(0) for take in takes)

    qk = nt(normed, w_qk).astype(BF16)
    values = nt(normed, w_val).astype(BF16)
    sums, local, future, ends = chunk_states(qk, values, gate_in, heads)
    w_og_all, w_out_all = (take.join(1, ends) for take in takes)
    later = neighbour_future(future[:, 0], True)
    incoming = exchange_states(ends, False)
    outgate = nt(normed, w_og_all)
    gain_group = group_gain.astype(F32)[None, :]
    mixed, gated = mix(flags, qk, values, sums, local, incoming, future, later, outgate, gain_group)
    resid = inputs + nn(gated, w_out_all)
    scale_two = rms_scale(resid)
    normed_two = (resid * scale_two * gain_two).astype(BF16)

    side = width // 2
    feed, d_norm_two, grads_ffn, near_down, far_down = feed_forward(
        order, ffn_all, normed_two, upstream
    )
    grads_ffn = scatter_units(grads_ffn)
    fast = split_axes()
    pairs = heads // 2
    give_down = [BlockScatter("ctx"), BlockScatter("dpo")]
    received_down = swapped(far_down, "core") if fast else None

    def step_down(step, *args):
        return [getattr(one, step)(*args) for one in give_down] if fast else []

    grad_ffn_term = jnp.sum(d_norm_two * resid * scale_two, axis=0, keepdims=True)
    d_resid = upstream.astype(F32) + norm_back(d_norm_two, resid, scale_two, gain_two)
    d_branch = d_resid.astype(BF16)
    d_gated = nt(d_branch, w_out_all)
    d_outgate, d_mixed, gain_terms, back_local, back_ends, earlier = gate_back(
        flags, d_gated, outgate, mixed, gain_group, qk, sums, heads
    )
    grad_group_term = jnp.sum(gain_terms, axis=0)
    if fast:
        near_late = tie(near_down, d_outgate)
        for i in range(2):
            cut = slice(i * pairs, (i + 1) * pairs)
            give_down[i].one(near_late[:, cut], received_down[:, cut])
    earlier = neighbour_future(earlier, False)
    back_incoming = exchange_states(back_ends, True)
    far_out, far_gate = (
        tn(left, right[:, side:]).astype(BF16) for left, right in ((gated, d_branch), (d_outgate, normed))
    )
    near_out, near_gate = tn(gated, d_branch[:, :side]), tn(d_outgate, normed[:, :side])
    d_mixed = tie(
        d_mixed, far_out, far_gate, near_out, near_gate, *[one.sent for one in give_down if fast]
    )
    d_qk, d_val, d_gate_in = mix_back(
        flags, d_mixed, qk, values, sums, local, incoming, future, later, back_local, back_incoming, earlier, gate_in
    )
    give = [Scatter("ctx"), Scatter("dpo")]
    far_in = [tn(left, normed[:, side:]).astype(BF16) for left in (d_val, d_qk)]
    far_in = [
        give[0].core(jnp.concatenate([far_out, far_in[0]], axis=0)),
        give[1].core(jnp.concatenate([far_gate, far_in[1]], axis=0)),
    ]
    second_down = step_down("two", *far_in)
    d_gate_in = tie(d_gate_in, *far_in)
    grad_bias_here = jnp.sum(d_gate_in.astype(F32), axis=0, keepdims=True)
    grad_rank_here = tn(rank_low, d_gate_in)
    d_rank_low = nt(d_gate_in, rank_out).astype(BF16)
    d_tied = tie((d_qk, d_val), *second_down, grad_rank_here, d_rank_low)
    near_in = [
        give[0].one([near_out, tn(d_tied[1], normed[:, :side])]),
        give[1].one([near_gate, tn(d_tied[0], normed[:, :side])]),
    ]
    d_low = tie((d_qk, d_val, d_outgate), *near_in)
    d_normed = nn(d_low[0], w_qk) + nn(d_low[1], w_val) + nn(d_low[2], w_og_all) + nn(d_rank_low, rank_in)
    grad_rank_in_term = tn(d_rank_low, normed)
    grad_in, small = pl.pallas_call(
        functools.partial(finish_kernel, heads),
        in_specs=[smem()] + [pl.BlockSpec(memory_space=pltpu.VMEM)] * 9,
        out_specs=[pl.BlockSpec(memory_space=pltpu.VMEM)] * 2,
        out_shape=[shaped((length, width), F32), shaped((256, 128), F32)],
        scratch_shapes=[pltpu.VMEM((CHUNK, width), F32)],
        compiler_params=params(),
        name="finish",
    )(
        order,
        d_resid,
        d_normed,
        inputs_low,
        gain_one,
        grad_rank_in_term,
        grad_rank_here,
        grad_bias_here,
        grad_group_term,
        grad_ffn_term,
    )
    sums_down = step_down("sums", *near_in)
    if fast:
        slots_down = jnp.concatenate(sums_down, axis=0)
        parts_down = lax.all_to_all(slots_down, "tp", 0, 0, tiled=True)
        grad_down = add_slots([parts_down[k] for k in range(heads)])
    else:
        parts_down = ()
        slots_down = jnp.concatenate([near_down, far_down], axis=0)
        slots_down = jnp.transpose(slots_down, (1, 2, 0, 3)).reshape(heads, units, width)
        grad_down = lax.psum_scatter(slots_down.astype(F32), "tp", scatter_dimension=0, tiled=True)
        grad_down = add_slots([grad_down[0]])
    hops = [one.two() for one in give]
    parts = [one.sums(parts_down).reshape(2, heads, DV, -1) for one in give]
    slots_in = [[parts[0][0, k], parts[1][0, k], parts[1][1, k], parts[0][1, k]] for k in range(heads)]
    hidden_out = call_whole(
        output_kernel, [order], [resid, feed], [shaped((length, width), BF16)], "output"
    )[0][None]
    grads_ffn = grads_ffn.astype(F32)
    grad_gate, grad_up = grads_ffn[:units].T, grads_ffn[units : 2 * units].T
    if not fast:
        small = lax.psum(small, ("dpo", "core", "ctx", "tp"))
        mixer = add_slots(send_slots([jnp.concatenate(slot, axis=0) for slot in slots_in]))
        small = small.reshape(8, 32, 128)
        flat = lambda row: small[:, row].reshape(width)
        return (
            hidden_out,
            grad_in[None],
            flat(24),
            mixer[2 * DV : 2 * DV + DK].T,
            mixer[2 * DV + DK : 3 * DV].T,
            mixer[3 * DV :].T,
            mixer[DV : 2 * DV].T,
            jnp.swapaxes(small[:, :RANK], 1, 2).reshape(width, RANK),
            jnp.transpose(small[:, 16:24].reshape(2, heads, 8, DK), (0, 2, 1, 3)).reshape(RANK, -1),
            flat(26)[: heads * DK],
            flat(26)[heads * DK : heads * DK + DV],
            mixer[:DV],
            flat(25),
            grad_gate,
            grad_up,
            grad_down,
        )
    small = sum_here(tie(small, *hops)).astype(BF16)
    parts_in = send_slots([jnp.concatenate([*slot, small], axis=0) for slot in slots_in])
    parts_in[0] = tie(parts_in[0], grad_gate, grad_up, grad_down, hidden_out)
    vmem = pl.BlockSpec(memory_space=pltpu.VMEM)
    shapes = [
        (128, DK),
        (128, DK),
        (128, DV),
        (128, DV),
        (DV, 128),
        (1, width),
        (RANK, width),
        (RANK, heads * DK),
        (1, heads * DK),
        (1, DV),
        (1, width),
    ]
    last = pl.pallas_call(
        functools.partial(last_kernel, heads, heads),
        in_specs=[smem()] + [vmem] * heads,
        out_specs=[vmem] * len(shapes),
        out_shape=[shaped(shape, F32) for shape in shapes],
        scratch_shapes=[pltpu.VMEM((heads, 256, 128), F32)],
        compiler_params=params(),
        name="last",
    )(order, *parts_in)
    grad_query, grad_key, grad_value, grad_outgate, grad_output = last[:5]
    return (
        hidden_out,
        grad_in[None],
        last[5][0],
        grad_query,
        grad_key,
        grad_value,
        grad_outgate,
        last[6].T,
        last[7],
        last[8][0],
        last[9][0],
        grad_output,
        last[10][0],
        grad_gate,
        grad_up,
        grad_down,
    )


def solution(mesh):
    sizes = dict(mesh.shape)
    cores = 2
    inner = Mesh(
        mesh.devices.reshape(sizes["dp"] // cores, cores, sizes["ctx"], sizes["tp"]),
        ("dpo", "core", "ctx", "tp"),
    )
    dp = ("dpo", "core")
    tokens = P(dp, ("ctx", "tp"), None)
    columns = P((*dp, "ctx"), "tp")
    rows = P("tp", (*dp, "ctx"))
    return jax.shard_map(
        on_device,
        mesh=inner,
        in_specs=(
            tokens,
            tokens,
            P(dp, None),
            P(),
            columns,
            columns,
            columns,
            columns,
            P(),
            P(),
            P(),
            P(),
            rows,
            P(),
            columns,
            columns,
            rows,
        ),
        out_specs=(
            tokens,
            tokens,
            P(),
            columns,
            columns,
            columns,
            columns,
            P(),
            P(),
            P(),
            P(),
            rows,
            P(),
            columns,
            columns,
            rows,
        ),
        check_vma=False,
    )
```

```python
import functools

import jax
import jax.numpy as jnp
from jax import lax
from jax.experimental import pallas as pl
from jax.experimental.pallas import tpu as pltpu
from jax.sharding import Mesh, PartitionSpec as P

DK = 128
DV = 256
RANK = 16
PIECE = 256
CHUNK = 128
EPSILON = 1e-06
GATE_NORM = 16.0
F32 = jnp.float32
BF16 = jnp.bfloat16
VMEM_LIMIT = 60 * 1024 * 1024


def nn(left, right):
    return lax.dot_general(left, right, (((1,), (0,)), ((), ())), preferred_element_type=F32)


def nt(left, right):
    return lax.dot_general(left, right, (((1,), (1,)), ((), ())), preferred_element_type=F32)


def tn(left, right):
    return lax.dot_general(left, right, (((0,), (0,)), ((), ())), preferred_element_type=F32)


def iota2(axis):
    return lax.broadcasted_iota(jnp.int32, (CHUNK, CHUNK), axis)


def split_dot(matrix, values, terms):
    total = None
    for _ in range(terms):
        part = values.astype(BF16)
        values = values - part.astype(F32)
        product = nn(matrix, part)
        total = product if total is None else total + product
    return total


def state_rows(state, log_decay):
    high = log_decay.astype(BF16).astype(F32)
    rows = lax.broadcasted_iota(jnp.int32, (16, DK), 0)
    extra = jnp.where(rows == 0, high, jnp.where(rows == 1, log_decay - high, 0.0))
    return jnp.concatenate([state, extra], axis=0).astype(BF16)


def states_kernel(chunks, qk_ref, value_ref, gate_ref, sums_ref, local_ref, future_ref, end_ref):
    lower = (iota2(0) >= iota2(1)).astype(BF16)
    state = jnp.zeros((DV, DK), F32)
    total = jnp.zeros((1, DK), F32)
    for j in range(chunks):
        rows = pl.ds(j * CHUNK, CHUNK)
        gate_in = gate_ref[rows, :]
        gate_log = (jnp.minimum(gate_in, 0.0) - jnp.log1p(jnp.exp(-jnp.abs(gate_in)))) * (
            1.0 / GATE_NORM
        )
        sums = split_dot(lower, gate_log, 3)
        sums_ref[rows, :] = sums
        last = sums[CHUNK - 1 : CHUNK, :]
        key_rows = qk_ref[rows, DK:].astype(F32)
        value_rows = value_ref[rows, :]
        local_ref[0, j] = state
        both = jnp.concatenate(
            [(key_rows * jnp.exp(last - sums)).astype(BF16), (key_rows * jnp.exp(sums)).astype(BF16)],
            axis=1,
        )
        update = tn(value_rows, both)
        state = state * jnp.exp(last) + update[:, :DK]
        total = total + last
        future_ref[0, j] = update[:, DK:].astype(BF16)
    end_ref[0] = state_rows(state, total)


def scores_of(queries, key_rows, sums, pic):
    middle = sums[CHUNK // 2 - 1 : CHUNK // 2, :]
    grow = jnp.exp(sums - middle)
    shrink = jnp.exp(middle - sums)
    q1 = (queries * grow).astype(BF16)
    k1 = (key_rows * shrink).astype(BF16)
    q2 = (queries * shrink).astype(BF16)
    k2 = (key_rows * grow).astype(BF16)
    row, col = iota2(0), iota2(1)
    diagonal = jnp.sum(queries * key_rows, axis=1, keepdims=True)
    above = jnp.logical_and(row < col, pic > 0)
    scores = jnp.where(
        row > col,
        nt(q1, k1),
        jnp.where(row == col, diagonal, jnp.where(above, nt(q2, k2), 0.0)),
    )
    return scores, q1, k1, q2, k2, grow, shrink, above


def mix_kernel(
    chunks,
    flags_ref,
    qk_ref,
    value_ref,
    sums_ref,
    local_ref,
    incoming_ref,
    future_ref,
    later_ref,
    outgate_ref,
    gain_ref,
    mixed_ref,
    gated_ref,
):
    incoming = incoming_ref[0].astype(F32)
    before = jnp.zeros((1, DK), F32)
    gain = gain_ref[...]
    for j in range(chunks):
        rows = pl.ds(j * CHUNK, CHUNK)
        sums = sums_ref[rows, :]
        last = sums[CHUNK - 1 : CHUNK, :]
        queries = qk_ref[rows, :DK].astype(F32) * DK**-0.5
        key_rows = qk_ref[rows, DK:].astype(F32)
        value_rows = value_ref[rows, :]
        scores = scores_of(queries, key_rows, sums, flags_ref[0, j])[0]
        state = (local_ref[0, j] + incoming * jnp.exp(before)).astype(BF16)
        later = later_ref[0] if j == chunks - 1 else future_ref[0, j + 1]
        cross = flags_ref[1, j].astype(F32)
        factors = jnp.concatenate(
            [
                (queries * jnp.exp(sums)).astype(BF16),
                (queries * (jnp.exp(last - sums) * cross)).astype(BF16),
            ],
            axis=1,
        )
        mixed = nn(scores.astype(BF16), value_rows) + nt(
            factors, jnp.concatenate([state, later], axis=1)
        )
        before = before + last
        mixed_ref[rows, :] = mixed
        scale = lax.rsqrt(jnp.mean(mixed * mixed, axis=1, keepdims=True) + EPSILON)
        gate = outgate_ref[rows, :]
        gated_ref[rows, :] = (mixed * scale * gain * gate * jax.nn.sigmoid(gate)).astype(BF16)


def gate_back_kernel(
    chunks,
    flags_ref,
    d_gated_ref,
    outgate_ref,
    mixed_ref,
    gain_ref,
    qk_ref,
    sums_ref,
    d_outgate_ref,
    d_mixed_ref,
    gain_grad_ref,
    local_ref,
    end_ref,
    earlier_ref,
):
    gain = gain_ref[...]
    state = jnp.zeros((DV, DK), F32)
    total = jnp.zeros((1, DK), F32)
    gain_grad = jnp.zeros((1, DV), F32)
    for j in reversed(range(chunks)):
        rows = pl.ds(j * CHUNK, CHUNK)
        d_gated = d_gated_ref[rows, :]
        gate = outgate_ref[rows, :]
        mixed = mixed_ref[rows, :]
        sigma = jax.nn.sigmoid(gate)
        scale = lax.rsqrt(jnp.mean(mixed * mixed, axis=1, keepdims=True) + EPSILON)
        unit = mixed * scale
        d_grouped = d_gated * gate * sigma
        slope = sigma * (1.0 + gate * (1.0 - sigma))
        d_outgate_ref[rows, :] = (d_gated * unit * gain * slope).astype(BF16)
        gain_grad = gain_grad + jnp.sum(d_grouped * unit, axis=0, keepdims=True)
        weighted = gain * d_grouped
        d_mixed = scale * (weighted - unit * jnp.mean(weighted * unit, axis=1, keepdims=True))
        d_low = d_mixed.astype(BF16)
        d_mixed_ref[rows, :] = d_low
        sums = sums_ref[rows, :]
        last = sums[CHUNK - 1 : CHUNK, :]
        queries = qk_ref[rows, :DK].astype(F32) * DK**-0.5
        local_ref[0, j] = state
        update = tn(d_low, (queries * jnp.exp(sums)).astype(BF16))
        if j == chunks - 1:
            cross = flags_ref[1, j].astype(F32)
            earlier_ref[0] = tn(
                d_low, (queries * (jnp.exp(last - sums) * cross)).astype(BF16)
            ).astype(BF16)
        state = state * jnp.exp(last) + update
        total = total + last
    gain_grad_ref[0] = gain_grad
    end_ref[0] = state_rows(state, total)


def mix_back_kernel(
    chunks,
    flags_ref,
    d_mixed_ref,
    qk_ref,
    value_ref,
    sums_ref,
    local_ref,
    incoming_ref,
    future_ref,
    later_ref,
    back_local_ref,
    back_incoming_ref,
    earlier_ref,
    gate_ref,
    d_qk_ref,
    d_value_ref,
    d_gate_ref,
):
    incoming = incoming_ref[0].astype(F32)
    back_incoming = back_incoming_ref[0].astype(F32)
    lasts = [sums_ref[pl.ds(j * CHUNK + CHUNK - 1, 1), :] for j in range(chunks)]
    row, col = iota2(0), iota2(1)
    upper = (row <= col).astype(BF16)
    before = jnp.zeros((1, DK), F32)
    d_future = earlier_ref[0]
    for j in range(chunks):
        rows = pl.ds(j * CHUNK, CHUNK)
        sums = sums_ref[rows, :]
        last = lasts[j]
        after = jnp.zeros((1, DK), F32)
        for l in range(j + 1, chunks):
            after = after + lasts[l]
        queries = qk_ref[rows, :DK].astype(F32) * DK**-0.5
        key_rows = qk_ref[rows, DK:].astype(F32)
        value_rows = value_ref[rows, :]
        d_mixed = d_mixed_ref[rows, :]
        scores, q1, k1, q2, k2, grow, shrink, above = scores_of(
            queries, key_rows, sums, flags_ref[0, j]
        )
        state = local_ref[0, j] + incoming * jnp.exp(before)
        back_state = back_local_ref[0, j] + back_incoming * jnp.exp(after)
        later = later_ref[0] if j == chunks - 1 else future_ref[0, j + 1]
        cross = flags_ref[1, j].astype(F32)
        from_start = jnp.exp(sums)
        to_end = jnp.exp(last - sums)
        to_later = to_end * cross
        d_scores = nt(d_mixed, value_rows)
        on_diagonal = jnp.sum(jnp.where(row == col, d_scores, 0.0), axis=1, keepdims=True)
        below = jnp.where(row > col, d_scores, 0.0).astype(BF16)
        ahead = jnp.where(above, d_scores, 0.0).astype(BF16)
        dq_causal = grow * nn(below, k1)
        dk_causal = shrink * tn(below, q1)
        dq_ahead = shrink * nn(ahead, k2)
        dk_ahead = grow * tn(ahead, q2)
        d_factors = nn(d_mixed, jnp.concatenate([state.astype(BF16), later], axis=1))
        dq_causal = dq_causal + from_start * d_factors[:, :DK]
        dq_later = to_later * d_factors[:, DK:]
        back_pair = jnp.concatenate([back_state.astype(BF16), d_future], axis=1)
        d_factors = nn(value_rows, back_pair)
        dk_state = to_end * d_factors[:, :DK]
        dk_earlier = from_start * d_factors[:, DK:]
        key_factors = jnp.concatenate(
            [(key_rows * to_end).astype(BF16), (key_rows * from_start).astype(BF16)], axis=1
        )
        d_values = tn(scores.astype(BF16), d_mixed) + nt(key_factors, back_pair)
        d_future = tn(d_mixed, (queries * to_later).astype(BF16)).astype(BF16)
        d_sums = queries * (dq_causal - dq_ahead - dq_later) + key_rows * (
            dk_ahead + dk_earlier - dk_causal - dk_state
        )
        d_last = (
            jnp.sum(key_rows * dk_state + queries * dq_later, axis=0, keepdims=True)
            + jnp.sum(state * back_state, axis=0, keepdims=True) * jnp.exp(last)
        )
        d_log = split_dot(upper, d_sums, 2) + d_last
        gate_in = gate_ref[rows, :]
        d_gate_ref[rows, :] = (d_log * jax.nn.sigmoid(-gate_in) * (1.0 / GATE_NORM)).astype(BF16)
        d_qk_ref[rows, :DK] = (
            (dq_causal + dq_ahead + dq_later + on_diagonal * key_rows) * DK**-0.5
        ).astype(BF16)
        d_qk_ref[rows, DK:] = (
            dk_causal + dk_ahead + dk_state + dk_earlier + on_diagonal * queries
        ).astype(BF16)
        d_value_ref[rows, :] = d_values.astype(BF16)
        before = before + last


def rows_block(length, width):
    return pl.BlockSpec((length, width), lambda h: (0, h))


def lead_block(*inner):
    return pl.BlockSpec((1, *inner), lambda h: (h,) + (0,) * len(inner))


def whole_block(*dims):
    return pl.BlockSpec(dims, lambda h: (0,) * len(dims))


def smem():
    return pl.BlockSpec(memory_space=pltpu.SMEM)


def params():
    return pltpu.CompilerParams(vmem_limit_bytes=VMEM_LIMIT)


def shaped(shape, kind):
    return jax.ShapeDtypeStruct(shape, kind)


def chunk_states(qk, values, gate_in, heads):
    length = qk.shape[0]
    chunks = length // CHUNK
    return pl.pallas_call(
        functools.partial(states_kernel, chunks),
        grid=(heads,),
        in_specs=[rows_block(length, 2 * DK), rows_block(length, DV), rows_block(length, DK)],
        out_specs=[
            rows_block(length, DK),
            lead_block(chunks, DV, DK),
            lead_block(chunks, DV, DK),
            lead_block(DV + 16, DK),
        ],
        out_shape=[
            shaped((length, heads * DK), F32),
            shaped((heads, chunks, DV, DK), F32),
            shaped((heads, chunks, DV, DK), BF16),
            shaped((heads, DV + 16, DK), BF16),
        ],
        compiler_params=params(),
        name="chunk_states",
    )(qk, values, gate_in)


def mix(flags, qk, values, sums, local, incoming, future, later, outgate, gain):
    length = qk.shape[0]
    heads, chunks = local.shape[:2]
    return pl.pallas_call(
        functools.partial(mix_kernel, chunks),
        grid=(heads,),
        in_specs=[
            smem(),
            rows_block(length, 2 * DK),
            rows_block(length, DV),
            rows_block(length, DK),
            lead_block(chunks, DV, DK),
            lead_block(DV, DK),
            lead_block(chunks, DV, DK),
            lead_block(DV, DK),
            rows_block(length, DV),
            whole_block(1, DV),
        ],
        out_specs=[rows_block(length, DV), rows_block(length, DV)],
        out_shape=[shaped((length, heads * DV), F32), shaped((length, heads * DV), BF16)],
        compiler_params=params(),
        name="mix",
    )(flags, qk, values, sums, local, incoming, future, later, outgate, gain)


def gate_back(flags, d_gated, outgate, mixed, gain, qk, sums, heads):
    length = qk.shape[0]
    chunks = length // CHUNK
    return pl.pallas_call(
        functools.partial(gate_back_kernel, chunks),
        grid=(heads,),
        in_specs=[
            smem(),
            rows_block(length, DV),
            rows_block(length, DV),
            rows_block(length, DV),
            whole_block(1, DV),
            rows_block(length, 2 * DK),
            rows_block(length, DK),
        ],
        out_specs=[
            rows_block(length, DV),
            rows_block(length, DV),
            lead_block(1, DV),
            lead_block(chunks, DV, DK),
            lead_block(DV + 16, DK),
            lead_block(DV, DK),
        ],
        out_shape=[
            shaped((length, heads * DV), BF16),
            shaped((length, heads * DV), BF16),
            shaped((heads, 1, DV), F32),
            shaped((heads, chunks, DV, DK), F32),
            shaped((heads, DV + 16, DK), BF16),
            shaped((heads, DV, DK), BF16),
        ],
        compiler_params=params(),
        name="gate_back",
    )(flags, d_gated, outgate, mixed, gain, qk, sums)


def mix_back(
    flags, d_mixed, qk, values, sums, local, incoming, future, later, back_local, back_incoming, earlier, gate_in
):
    length = qk.shape[0]
    heads, chunks = local.shape[:2]
    return pl.pallas_call(
        functools.partial(mix_back_kernel, chunks),
        grid=(heads,),
        in_specs=[
            smem(),
            rows_block(length, DV),
            rows_block(length, 2 * DK),
            rows_block(length, DV),
            rows_block(length, DK),
            lead_block(chunks, DV, DK),
            lead_block(DV, DK),
            lead_block(chunks, DV, DK),
            lead_block(DV, DK),
            lead_block(chunks, DV, DK),
            lead_block(DV, DK),
            lead_block(DV, DK),
            rows_block(length, DK),
        ],
        out_specs=[rows_block(length, 2 * DK), rows_block(length, DV), rows_block(length, DK)],
        out_shape=[
            shaped((length, heads * 2 * DK), BF16),
            shaped((length, heads * DV), BF16),
            shaped((length, heads * DK), BF16),
        ],
        compiler_params=params(),
        name="mix_back",
    )(
        flags, d_mixed, qk, values, sums, local, incoming, future, later, back_local, back_incoming, earlier, gate_in
    )


def chain_kernel(count, backwards, place_ref, *refs):
    parts, other_ref, total_ref = refs[:count], refs[count], refs[count + 1]
    outs, scratch, result = refs[count + 2 : 2 * count + 2], refs[-2], refs[-1]
    place, joined = place_ref[0], place_ref[1]
    for k in range(count):
        scratch[lax.rem(place + k, count)] = parts[k][...].astype(F32)
    state = jnp.where(joined > 0, other_ref[:DV, :].astype(F32), 0.0)
    for z in reversed(range(count)) if backwards else range(count):
        result[z] = state.astype(BF16)
        log_decay = scratch[z, DV : DV + 1, :] + scratch[z, DV + 1 : DV + 2, :]
        state = state * jnp.exp(log_decay) + scratch[z, :DV, :]
    total_ref[...] = state.astype(BF16)
    for k in range(count):
        outs[k][...] = result[lax.rem(place + k, count)]


def chain(parts, other, place, joined, backwards):
    count = len(parts)
    return pl.pallas_call(
        functools.partial(chain_kernel, count, backwards),
        in_specs=[smem()] + [pl.BlockSpec(memory_space=pltpu.VMEM)] * (count + 1),
        out_specs=[pl.BlockSpec(memory_space=pltpu.VMEM)] * (count + 1),
        out_shape=[shaped((DV, DK), BF16)] * (count + 1),
        scratch_shapes=[
            pltpu.VMEM((count, DV + 16, DK), F32),
            pltpu.VMEM((count, DV, DK), BF16),
        ],
        compiler_params=params(),
        name="chain",
    )(jnp.stack([place, joined]).astype(jnp.int32), *parts, other)


def shifted(array, axis, by):
    size = lax.axis_size(axis)
    return lax.ppermute(array, axis, [(i, (i + by) % size) for i in range(size)])


def swapped(array, axis):
    return lax.ppermute(array, axis, [(0, 1), (1, 0)])


def exchange_states(ends, backwards):
    count = lax.axis_size("tp")
    place = lax.axis_index("tp")
    side = lax.axis_index("ctx")
    parts = [ends[0]] + [shifted(ends[k], "tp", -k) for k in range(1, count)]
    zero = jnp.zeros((DV, DK), BF16)
    total = chain(parts, zero, place, jnp.zeros_like(place), backwards)[0]
    other = swapped(total, "ctx")
    joined = (side == 0) if backwards else (side == 1)
    outs = chain(parts, other, place, joined.astype(place.dtype), backwards)[1:]
    return jnp.stack([outs[0]] + [shifted(outs[k], "tp", k) for k in range(1, count)])


def neighbour_future(first, odd_to_even):
    size = lax.axis_size("tp")
    if odd_to_even:
        moved = lax.ppermute(first, "tp", [(i + 1, i) for i in range(0, size - 1, 2)])
        return jnp.concatenate([moved[1:], moved[:1]], axis=0)
    moved = lax.ppermute(first, "tp", [(i, i + 1) for i in range(0, size - 1, 2)])
    return jnp.concatenate([moved[-1:], moved[:-1]], axis=0)


def take_columns(ref, order_ref, out_ref):
    for j in range(8):
        out_ref[:, j * 128 : (j + 1) * 128] = ref[:, pl.ds(pl.multiple_of(order_ref[j] * 128, 128), 128)]


def begin_kernel(
    heads,
    order_ref,
    hidden_ref,
    cot_ref,
    gain_one_ref,
    gain_two_ref,
    rank_in_ref,
    rank_out_ref,
    bias_ref,
    inputs_ref,
    upstream_ref,
    normed_ref,
    new_one_ref,
    new_two_ref,
    new_rank_in_ref,
    new_rank_out_ref,
    new_bias_ref,
):
    take_columns(gain_one_ref, order_ref, new_one_ref)
    take_columns(gain_two_ref, order_ref, new_two_ref)
    take_columns(rank_in_ref, order_ref, new_rank_in_ref)
    for k in range(heads):
        lanes = pl.ds(pl.multiple_of(order_ref[16 + k] * DK, DK), DK)
        new_rank_out_ref[:, k * DK : (k + 1) * DK] = rank_out_ref[:, lanes]
        new_bias_ref[:, k * DK : (k + 1) * DK] = bias_ref[:, lanes]
    take_columns(cot_ref, order_ref, upstream_ref)
    take_columns(hidden_ref, order_ref, inputs_ref)
    for i in range(hidden_ref.shape[0] // CHUNK):
        rows = pl.ds(i * CHUNK, CHUNK)
        values = inputs_ref[rows, :].astype(F32)
        scale = lax.rsqrt(jnp.mean(values * values, axis=1, keepdims=True) + EPSILON)
        normed_ref[rows, :] = (values * scale * new_one_ref[...]).astype(BF16)


def call_whole(kernel, smem_args, args, outs, name):
    vmem = pl.BlockSpec(memory_space=pltpu.VMEM)
    return pl.pallas_call(
        kernel,
        in_specs=[smem()] * len(smem_args) + [vmem] * len(args),
        out_specs=[vmem] * len(outs),
        out_shape=outs,
        compiler_params=params(),
        name=name,
    )(*smem_args, *args)


def pack_kernel(q_ref, k_ref, v_ref, g_ref, o_ref, gate_ref, up_ref, down_ref, mixer_ref, ffn_ref):
    at = 0
    for ref in (q_ref, k_ref, g_ref, v_ref):
        for i in range(ref.shape[1] // 128):
            mixer_ref[at : at + 128, :] = ref[:, i * 128 : (i + 1) * 128].T
            at += 128
    mixer_ref[at:, :] = o_ref[...]
    units = down_ref.shape[0]
    for i, ref in enumerate((gate_ref, up_ref)):
        ffn_ref[i * units : (i + 1) * units, :] = ref[...]
    ffn_ref[2 * units :, :] = down_ref[...]


def pack_weights(w_query, w_key, w_value, w_outgate, w_output, w_gate, w_up, w_down):
    if not split_axes():
        mixer = [w_query.T, w_key.T, w_outgate.T, w_value.T, w_output]
        return jnp.concatenate(mixer, axis=0), jnp.concatenate([w_gate.T, w_up.T, w_down], axis=0)
    args = (w_query, w_key, w_value, w_outgate, w_output, w_gate.T, w_up.T, w_down)
    rows = 2 * DK + 3 * DV
    return call_whole(
        pack_kernel,
        [],
        args,
        [shaped((rows, 128), BF16), shaped((3 * w_down.shape[0], 128), BF16)],
        "pack",
    )


def output_kernel(back_ref, resid_ref, feed_ref, out_ref):
    for j in range(8):
        lanes = pl.ds(pl.multiple_of(back_ref[8 + j] * 128, 128), 128)
        out_ref[:, j * 128 : (j + 1) * 128] = (resid_ref[:, lanes] + feed_ref[:, lanes]).astype(BF16)


def finish_kernel(heads, back_ref, d_resid_ref, d_normed_ref, inputs_ref, gain_ref, rank_in_ref, rank_out_ref,
                  bias_ref, group_ref, ffn_ref, grad_ref, small_ref, scratch):
    gain = gain_ref[...]
    total = jnp.zeros((1, gain.shape[1]), F32)
    for i in range(inputs_ref.shape[0] // CHUNK):
        rows = pl.ds(i * CHUNK, CHUNK)
        values = inputs_ref[rows, :].astype(F32)
        scale = lax.rsqrt(jnp.mean(values * values, axis=1, keepdims=True) + EPSILON)
        unit = values * scale
        upstream = d_normed_ref[rows, :]
        total = total + jnp.sum(upstream * unit, axis=0, keepdims=True)
        weighted = upstream * gain
        scratch[0:CHUNK, :] = d_resid_ref[rows, :] + scale * (
            weighted - unit * jnp.mean(weighted * unit, axis=1, keepdims=True)
        )
        for j in range(8):
            lanes = pl.ds(pl.multiple_of(back_ref[8 + j] * 128, 128), 128)
            grad_ref[rows, j * 128 : (j + 1) * 128] = scratch[0:CHUNK, lanes]
    small_ref[...] = jnp.zeros_like(small_ref)
    scratch[0:16, :] = rank_in_ref[...]
    scratch[24:25, :] = total
    scratch[25:26, :] = ffn_ref[...]
    for j in range(8):
        lanes = pl.ds(pl.multiple_of(back_ref[8 + j] * 128, 128), 128)
        small_ref[j * 32 : j * 32 + 16, :] = scratch[0:16, lanes]
        small_ref[j * 32 + 24 : j * 32 + 26, :] = scratch[24:26, lanes]
    for k in range(heads):
        lanes = pl.ds(pl.multiple_of(back_ref[16 + k] * DK, DK), DK)
        small_ref[k * 32 + 16 : k * 32 + 24, :] = rank_out_ref[0:8, lanes]
        small_ref[(heads + k) * 32 + 16 : (heads + k) * 32 + 24, :] = rank_out_ref[8:16, lanes]
        small_ref[k * 32 + 26 : k * 32 + 27, :] = bias_ref[:, lanes]
    for k in range(DV // 128):
        small_ref[(heads + k) * 32 + 26 : (heads + k) * 32 + 27, :] = group_ref[:, k * 128 : (k + 1) * 128]


def last_kernel(heads, count, order_ref, *refs):
    parts, outs, scratch = refs[:count], refs[count:-1], refs[-1]
    q_ref, k_ref, v_ref, g_ref, o_ref, mixer_ref, in_ref, out_ref, bias_ref, group_ref, ffn_ref = outs
    small = 4 * DV

    def summed(at, rows):
        total = parts[0][at : at + rows, :].astype(F32)
        for part in parts[1:]:
            total = total + part[at : at + rows, :].astype(F32)
        return total

    o_ref[...] = summed(0, DV)
    at = DV
    for ref in (g_ref, q_ref, k_ref, v_ref):
        for i in range(ref.shape[1] // 128):
            ref[:, i * 128 : (i + 1) * 128] = summed(at, 128).T
            at += 128
    for k in range(count):
        scratch[k] = parts[k][small:, :].astype(F32)
    total = scratch[order_ref[16]]
    for z in range(1, count):
        total = total + scratch[order_ref[16 + z]]
    for j in range(8):
        lanes = slice(j * 128, (j + 1) * 128)
        block = total[j * 32 : (j + 1) * 32]
        in_ref[:, lanes] = block[0:16]
        mixer_ref[:, lanes] = block[24:25]
        ffn_ref[:, lanes] = block[25:26]
        k = j % heads
        out_ref[(j // heads) * 8 : (j // heads) * 8 + 8, k * DK : (k + 1) * DK] = block[16:24]
        if j < heads:
            bias_ref[:, lanes] = block[26:27]
        elif j < heads + DV // 128:
            group_ref[:, k * 128 : (k + 1) * 128] = block[26:27]


def split_axes():
    return all(lax.axis_size(axis) == 2 for axis in ("dpo", "core", "ctx"))


def column_order():
    heads = lax.axis_size("tp")
    place = lax.axis_index("tp")
    order, back = list(range(8)), list(range(8))
    if split_axes():
        y, core, x = (lax.axis_index(axis) for axis in ("dpo", "core", "ctx"))
        for j in range(8):
            high, middle, last = j >> 2, (j >> 1) & 1, j & 1
            order[j] = ((y ^ middle) * 2 + (core ^ high)) * 2 + (x ^ last)
            back[j] = ((core ^ middle) * 2 + (y ^ high)) * 2 + (x ^ last)
    slots = [lax.rem(place - k + heads, heads) for k in range(heads)]
    return jnp.stack([jnp.asarray(v, jnp.int32) for v in order + back + slots])


def tie(array, *others):
    others = [other for other in others if other is not None]
    return lax.optimization_barrier((array, *others))[0] if others else array


def weight_axes(first):
    return ("ctx", "dpo") if first == "ctx" else ("dpo", "ctx")


def join_kernel(swap, *refs):
    out = refs[-1]
    for i in range(4):
        for half in range(2):
            block = 4 * (i // 2) + (2 * half + i % 2 if swap else 2 * (i % 2) + half)
            out[:, block * 128 : (block + 1) * 128] = refs[2 * i + half][...]


def join_columns(pieces, swap, part):
    rows = pieces[0].shape[0] // 4
    tile = 512
    specs, args = [], []
    for piece in pieces:
        for half in range(2):
            start = (2 * half + part) * (rows // tile)
            specs.append(pl.BlockSpec((tile, 128), functools.partial(lambda at, i: (at + i, 0), start)))
            args.append(piece)
    return pl.pallas_call(
        functools.partial(join_kernel, swap),
        grid=(rows // tile,),
        in_specs=specs,
        out_specs=pl.BlockSpec((tile, 1024), lambda i: (i, 0)),
        out_shape=shaped((rows, 1024), pieces[0].dtype),
        compiler_params=params(),
        name="join",
    )(*args)


def ffn_kernel(
    units,
    order_ref,
    every_ref,
    rows_ref,
    upstream_ref,
    feed_ref,
    d_rows_ref,
    grads_ref,
    near_ref,
    far_ref,
    weights,
    lefts,
):
    rows, upstream = rows_ref[...], upstream_ref[...]
    for j in range(8):
        weights[:, j * 128 : (j + 1) * 128] = every_ref[order_ref[j], 0]
    both, down = weights[: 2 * units, :], weights[2 * units :, :]
    gate_pre = nt(weights[:units, :], rows)
    sigma = jax.nn.sigmoid(gate_pre)
    silu = gate_pre * sigma
    slope = sigma * (1.0 + gate_pre * (1.0 - sigma))
    up_pre = nt(weights[units : 2 * units, :], rows)
    d_act = nt(down, upstream)
    lefts[2 * units :, :] = (silu * up_pre).astype(BF16)
    lefts[:units, :] = (d_act * up_pre * slope).astype(BF16)
    lefts[units : 2 * units, :] = (d_act * silu).astype(BF16)
    d_rows = tn(lefts[: 2 * units, :], both)
    feed = tn(lefts[2 * units :, :], down)

    @pl.when(pl.program_id(0) == 0)
    def _():
        d_rows_ref[...] = d_rows
        feed_ref[...] = feed

    @pl.when(pl.program_id(0) > 0)
    def _():
        d_rows_ref[...] += d_rows
        feed_ref[...] += feed

    for pair in range(4):
        lanes = slice(pair * 256, (pair + 1) * 256)
        grads_in = nn(lefts[: 2 * units, :], rows[:, lanes]).astype(BF16)
        grads_down = nn(lefts[2 * units :, :], upstream[:, lanes]).astype(BF16)
        down_ref = near_ref if pair < 2 else far_ref
        for j in range(2):
            block = order_ref[2 * pair + j]
            grads_ref[block, 0, : 2 * units, :] = grads_in[:, j * 128 : (j + 1) * 128]
            down_ref[2 * (pair % 2) + j, 0] = grads_down[:, j * 128 : (j + 1) * 128]
    padding = grads_ref.shape[2] - 2 * units
    if padding:
        grads_ref[:, 0, 2 * units :, :] = jnp.zeros((8, padding, 128), BF16)


def feed_forward(order, every, rows, upstream):
    length, width = rows.shape
    blocks, slots, total, _ = every.shape
    units = total // 3
    padded = -(-2 * units // 48) * 48
    whole = pl.BlockSpec((length, width), lambda t, order: (0, 0))
    half = pl.BlockSpec((4, 1, units, 128), lambda t, order: (0, t, 0, 0))
    return pl.pallas_call(
        functools.partial(ffn_kernel, units),
        grid_spec=pltpu.PrefetchScalarGridSpec(
            num_scalar_prefetch=1,
            grid=(slots,),
            in_specs=[
                pl.BlockSpec((blocks, 1, total, 128), lambda t, order: (0, t, 0, 0)),
                whole,
                whole,
            ],
            out_specs=[
                whole,
                whole,
                pl.BlockSpec((blocks, 1, padded, 128), lambda t, order: (0, t, 0, 0)),
                half,
                half,
            ],
            scratch_shapes=[pltpu.VMEM((total, width), BF16), pltpu.VMEM((total, length), BF16)],
        ),
        out_shape=[
            shaped((length, width), F32),
            shaped((length, width), F32),
            shaped((blocks, slots, padded, 128), BF16),
            shaped((4, slots, units, 128), BF16),
            shaped((4, slots, units, 128), BF16),
        ],
        compiler_params=params(),
        name="feed_forward",
    )(order, every, rows, upstream)


def gather_units(shard):
    count = lax.axis_size("tp")
    rows = shard.shape[0]
    if not split_axes():
        wide = lax.all_gather(shard, ("dpo", "core", "ctx"), axis=1, tiled=True)
        every = lax.all_gather(wide, "tp").reshape(count, rows, 8, 128)
        return jnp.transpose(every, (2, 0, 1, 3))
    every = lax.all_gather(shard, ("dpo", "core", "ctx", "tp"))
    return every.reshape(8, count, rows, 128)


def scatter_units(grads):
    blocks, count, rows, lanes = grads.shape
    if not split_axes():
        whole = jnp.transpose(grads, (1, 2, 0, 3)).reshape(count, rows, blocks * lanes)
        whole = lax.psum_scatter(whole, "tp", scatter_dimension=0, tiled=True)[0]
        return lax.psum_scatter(whole, ("dpo", "core", "ctx"), scatter_dimension=1, tiled=True)
    return lax.psum_scatter(
        grads.reshape(blocks * count, rows, lanes), ("dpo", "core", "ctx", "tp"), scatter_dimension=0
    )


def gather_slots(shard, sizes):
    count = lax.axis_size("tp")
    slots = [shard] + [shifted(shard, "tp", k) for k in range(1, count)]
    stacks, at = [], 0
    for size in sizes:
        stacks.append([slot[at : at + size] for slot in slots])
        at += size
    return stacks


class Gather:
    def __init__(self, stacks, first):
        self.first = weight_axes(first)
        self.stack = jnp.concatenate(sum(stacks, []), axis=0)

    def hop_one(self, *hold):
        own = tie(self.stack, *hold)
        if not split_axes():
            self.whole = lax.all_gather(own, ("dpo", "core", "ctx"), axis=1, tiled=True)
            return None
        self.own = own
        self.near = swapped(own, self.first[0])
        return self.near

    def hop_two(self, *hold):
        if not split_axes():
            return None
        self.pair = tie(jnp.concatenate([self.own, self.near], axis=0), *hold)
        self.far = swapped(self.pair, self.first[1])
        return self.far

    def hop_core(self):
        if split_axes():
            self.pieces = [
                self.pair, self.far, swapped(self.pair, "core"), swapped(self.far, "core")
            ]

    def join(self, part, *hold):
        if not split_axes():
            rows = self.whole.shape[0] // 2
            return self.whole[part * rows : (part + 1) * rows]
        pieces = [tie(self.pieces[0], *hold)] + self.pieces[1:]
        return join_columns(pieces, self.first[0] == "dpo", part)


class Scatter:
    def __init__(self, first):
        self.first = weight_axes(first)

    def core(self, far):
        self.sent = far
        if split_axes():
            self.received = swapped(far, "core")
        return far

    def one(self, nears):
        if not split_axes():
            near = jnp.concatenate(nears, axis=0)
            self.kept = jnp.concatenate([near, self.sent.astype(F32)], axis=-1)
            return None
        kept, sent, at = [], [], 0
        for near in nears:
            near = near + self.received[at : at + near.shape[0]].astype(F32)
            at += near.shape[0]
            quarter = near.shape[-1] // 4
            blocks = [near[:, i * quarter : (i + 1) * quarter] for i in range(4)]
            if self.first[0] == "ctx":
                mine, other = (blocks[0], blocks[2]), (blocks[1], blocks[3])
            else:
                mine, other = (blocks[0], blocks[1]), (blocks[2], blocks[3])
            kept.append(jnp.concatenate(mine, axis=-1).astype(BF16))
            sent.append(jnp.concatenate(other, axis=-1).astype(BF16))
        self.kept, self.sent = jnp.concatenate(kept, axis=0), jnp.concatenate(sent, axis=0)
        self.received = swapped(self.sent, self.first[0])
        return self.sent

    def two(self, *hold):
        if not split_axes():
            return None
        kept = tie(self.kept, *hold)
        quarter = kept.shape[-1] // 2
        sums = kept.astype(F32) + self.received.astype(F32)
        self.kept, self.sent = sums[..., :quarter].astype(BF16), sums[..., quarter:].astype(BF16)
        self.received = swapped(self.sent, self.first[1])
        return self.sent

    def sums(self, *hold):
        kept = tie(self.kept, *hold)
        if not split_axes():
            return kept
        return (kept.astype(F32) + self.received.astype(F32)).astype(BF16)


class BlockScatter(Scatter):
    def one(self, near, received):
        total = near.astype(F32) + received.astype(F32)
        one, two = ((0, 2), (1, 3)) if self.first[0] == "ctx" else ((0, 1), (2, 3))
        self.kept = jnp.stack([total[i] for i in one]).astype(BF16)
        self.sent = jnp.stack([total[i] for i in two]).astype(BF16)
        self.received = swapped(self.sent, self.first[0])
        return self.sent

    def two(self, *hold):
        kept = tie(self.kept, *hold)
        self.kept, self.sent = (
            (kept[i].astype(F32) + self.received[i].astype(F32)).astype(BF16) for i in range(2)
        )
        self.received = swapped(self.sent, self.first[1])
        return self.sent


def send_slots(slots):
    count = lax.axis_size("tp")
    return [slots[0]] + [shifted(slots[k], "tp", -k) for k in range(1, count)]


def add_slots(parts):
    total = parts[0].astype(F32)
    for part in parts[1:]:
        total = total + part.astype(F32)
    if not split_axes():
        total = lax.psum_scatter(
            total, ("dpo", "core", "ctx"), scatter_dimension=total.ndim - 1, tiled=True
        )
    return total


def sum_here(values):
    for axis in ("core", "ctx", "dpo"):
        values = values + swapped(values, axis)
    return values


def rms_scale(values):
    return lax.rsqrt(jnp.mean(values * values, axis=-1, keepdims=True) + EPSILON)


def norm_back(upstream, values, scale, gain):
    weighted = upstream * gain
    return scale * weighted - values * scale**3 * jnp.mean(
        weighted * values, axis=-1, keepdims=True
    )


def on_device(
    hidden_in,
    cotangent,
    pic_starts,
    norm_mixer,
    w_query,
    w_key,
    w_value,
    w_outgate,
    w_rank_in,
    w_rank_out,
    gate_bias,
    group_gain,
    w_output,
    norm_ffn,
    w_gate,
    w_up,
    w_down,
):
    seq_count, length, width = hidden_in.shape
    assert seq_count == 1 and width == 1024 and length % CHUNK == 0
    heads = lax.axis_size("tp")
    place = lax.axis_index("tp")
    chunks = length // CHUNK
    units = w_down.shape[0]

    mixer_shard, ffn_shard = pack_weights(
        w_query, w_key, w_value, w_outgate, w_output, w_gate, w_up, w_down
    )
    stacks = gather_slots(mixer_shard, [2 * DK, DV, DV, DV])
    takes = [Gather(stacks[:2], "dpo"), Gather(stacks[2:], "ctx")]
    order = column_order()
    ffn_all = gather_units(ffn_shard)
    kinds = [
        shaped((length, width), BF16),
        shaped((length, width), BF16),
        shaped((length, width), BF16),
        shaped((1, width), F32),
        shaped((1, width), F32),
        shaped((RANK, width), BF16),
        shaped((RANK, heads * DK), BF16),
        shaped((1, heads * DK), F32),
    ]
    inputs_low, upstream, normed, gain_one, gain_two, rank_in, rank_out, bias = call_whole(
        functools.partial(begin_kernel, heads),
        [order],
        [
            hidden_in[0],
            cotangent[0],
            norm_mixer.astype(F32)[None],
            norm_ffn.astype(F32)[None],
            w_rank_in.T,
            w_rank_out,
            gate_bias.astype(F32)[None],
        ],
        kinds,
        "begin",
    )
    inputs = inputs_low.astype(F32)

    part = lax.axis_index("ctx") * heads + place
    starts = part * length + jnp.arange(chunks, dtype=jnp.int32) * CHUNK
    inside = (starts[:, None] >= pic_starts[0][None, :]) & (
        starts[:, None] < pic_starts[0][None, :] + PIECE
    )
    in_piece = jnp.any(inside, axis=1)
    first_half = (starts % PIECE) == 0
    flags = jnp.stack([in_piece, in_piece & first_half]).astype(jnp.int32)

    rank_low = nt(normed, rank_in).astype(BF16)
    gate_in = nn(rank_low, rank_out) + bias
    first_hops = [take.hop_one() for take in takes]
    for take in takes:
        take.hop_two(*first_hops, gate_in)
    for take in takes:
        take.hop_core()
    w_qk, w_val = (take.join(0) for take in takes)

    qk = nt(normed, w_qk).astype(BF16)
    values = nt(normed, w_val).astype(BF16)
    sums, local, future, ends = chunk_states(qk, values, gate_in, heads)
    w_og_all, w_out_all = (take.join(1, ends) for take in takes)
    later = neighbour_future(future[:, 0], True)
    incoming = exchange_states(ends, False)
    outgate = nt(normed, w_og_all)
    gain_group = group_gain.astype(F32)[None, :]
    mixed, gated = mix(flags, qk, values, sums, local, incoming, future, later, outgate, gain_group)
    resid = inputs + nn(gated, w_out_all)
    scale_two = rms_scale(resid)
    normed_two = (resid * scale_two * gain_two).astype(BF16)

    side = width // 2
    feed, d_norm_two, grads_ffn, near_down, far_down = feed_forward(
        order, ffn_all, normed_two, upstream
    )
    grads_ffn = scatter_units(grads_ffn)
    fast = split_axes()
    pairs = heads // 2
    give_down = [BlockScatter("ctx"), BlockScatter("dpo")]
    received_down = swapped(far_down, "core") if fast else None

    def step_down(step, *args):
        return [getattr(one, step)(*args) for one in give_down] if fast else []

    grad_ffn_term = jnp.sum(d_norm_two * resid * scale_two, axis=0, keepdims=True)
    d_resid = upstream.astype(F32) + norm_back(d_norm_two, resid, scale_two, gain_two)
    d_branch = d_resid.astype(BF16)
    d_gated = nt(d_branch, w_out_all)
    d_outgate, d_mixed, gain_terms, back_local, back_ends, earlier = gate_back(
        flags, d_gated, outgate, mixed, gain_group, qk, sums, heads
    )
    grad_group_term = jnp.sum(gain_terms, axis=0)
    if fast:
        near_late = tie(near_down, d_outgate)
        for i in range(2):
            cut = slice(i * pairs, (i + 1) * pairs)
            give_down[i].one(near_late[:, cut], received_down[:, cut])
    earlier = neighbour_future(earlier, False)
    back_incoming = exchange_states(back_ends, True)
    far_out, far_gate = (
        tn(left, right[:, side:]).astype(BF16) for left, right in ((gated, d_branch), (d_outgate, normed))
    )
    d_mixed = tie(
        d_mixed, far_out, far_gate, *[one.sent for one in give_down if fast]
    )
    d_qk, d_val, d_gate_in = mix_back(
        flags, d_mixed, qk, values, sums, local, incoming, future, later, back_local, back_incoming, earlier, gate_in
    )
    give = [Scatter("ctx"), Scatter("dpo")]
    far_in = [tn(left, normed[:, side:]).astype(BF16) for left in (d_val, d_qk)]
    far_in = [
        give[0].core(jnp.concatenate([far_out, far_in[0]], axis=0)),
        give[1].core(jnp.concatenate([far_gate, far_in[1]], axis=0)),
    ]
    second_down = step_down("two", *far_in)
    d_gate_in = tie(d_gate_in, *far_in)
    grad_bias_here = jnp.sum(d_gate_in.astype(F32), axis=0, keepdims=True)
    grad_rank_here = tn(rank_low, d_gate_in)
    d_rank_low = nt(d_gate_in, rank_out).astype(BF16)
    d_tied = tie((d_qk, d_val), *second_down, grad_rank_here, d_rank_low)
    late = tie((gated, d_outgate), *far_in)
    near_out, near_gate = tn(late[0], d_branch[:, :side]), tn(late[1], normed[:, :side])
    near_in = [
        give[0].one([near_out, tn(d_tied[1], normed[:, :side])]),
        give[1].one([near_gate, tn(d_tied[0], normed[:, :side])]),
    ]
    d_low = tie((d_qk, d_val, d_outgate), *near_in)
    d_normed = nn(d_low[0], w_qk) + nn(d_low[1], w_val) + nn(d_low[2], w_og_all) + nn(d_rank_low, rank_in)
    grad_rank_in_term = tn(d_rank_low, normed)
    grad_in, small = pl.pallas_call(
        functools.partial(finish_kernel, heads),
        in_specs=[smem()] + [pl.BlockSpec(memory_space=pltpu.VMEM)] * 9,
        out_specs=[pl.BlockSpec(memory_space=pltpu.VMEM)] * 2,
        out_shape=[shaped((length, width), F32), shaped((256, 128), F32)],
        scratch_shapes=[pltpu.VMEM((CHUNK, width), F32)],
        compiler_params=params(),
        name="finish",
    )(
        order,
        d_resid,
        d_normed,
        inputs_low,
        gain_one,
        grad_rank_in_term,
        grad_rank_here,
        grad_bias_here,
        grad_group_term,
        grad_ffn_term,
    )
    sums_down = step_down("sums", *near_in)
    if fast:
        slots_down = jnp.concatenate(sums_down, axis=0)
        parts_down = lax.all_to_all(slots_down, "tp", 0, 0, tiled=True)
        grad_down = add_slots([parts_down[k] for k in range(heads)])
    else:
        parts_down = ()
        slots_down = jnp.concatenate([near_down, far_down], axis=0)
        slots_down = jnp.transpose(slots_down, (1, 2, 0, 3)).reshape(heads, units, width)
        grad_down = lax.psum_scatter(slots_down.astype(F32), "tp", scatter_dimension=0, tiled=True)
        grad_down = add_slots([grad_down[0]])
    hops = [one.two() for one in give]
    parts = [one.sums(parts_down).reshape(2, heads, DV, -1) for one in give]
    slots_in = [[parts[0][0, k], parts[1][0, k], parts[1][1, k], parts[0][1, k]] for k in range(heads)]
    hidden_out = call_whole(
        output_kernel, [order], [resid, feed], [shaped((length, width), BF16)], "output"
    )[0][None]
    grads_ffn = grads_ffn.astype(F32)
    grad_gate, grad_up = grads_ffn[:units].T, grads_ffn[units : 2 * units].T
    if not fast:
        small = lax.psum(small, ("dpo", "core", "ctx", "tp"))
        mixer = add_slots(send_slots([jnp.concatenate(slot, axis=0) for slot in slots_in]))
        small = small.reshape(8, 32, 128)
        flat = lambda row: small[:, row].reshape(width)
        return (
            hidden_out,
            grad_in[None],
            flat(24),
            mixer[2 * DV : 2 * DV + DK].T,
            mixer[2 * DV + DK : 3 * DV].T,
            mixer[3 * DV :].T,
            mixer[DV : 2 * DV].T,
            jnp.swapaxes(small[:, :RANK], 1, 2).reshape(width, RANK),
            jnp.transpose(small[:, 16:24].reshape(2, heads, 8, DK), (0, 2, 1, 3)).reshape(RANK, -1),
            flat(26)[: heads * DK],
            flat(26)[heads * DK : heads * DK + DV],
            mixer[:DV],
            flat(25),
            grad_gate,
            grad_up,
            grad_down,
        )
    small = sum_here(tie(small, *hops)).astype(BF16)
    parts_in = send_slots([jnp.concatenate([*slot, small], axis=0) for slot in slots_in])
    parts_in[0] = tie(parts_in[0], grad_gate, grad_up, grad_down, hidden_out)
    vmem = pl.BlockSpec(memory_space=pltpu.VMEM)
    shapes = [
        (128, DK),
        (128, DK),
        (128, DV),
        (128, DV),
        (DV, 128),
        (1, width),
        (RANK, width),
        (RANK, heads * DK),
        (1, heads * DK),
        (1, DV),
        (1, width),
    ]
    last = pl.pallas_call(
        functools.partial(last_kernel, heads, heads),
        in_specs=[smem()] + [vmem] * heads,
        out_specs=[vmem] * len(shapes),
        out_shape=[shaped(shape, F32) for shape in shapes],
        scratch_shapes=[pltpu.VMEM((heads, 256, 128), F32)],
        compiler_params=params(),
        name="last",
    )(order, *parts_in)
    grad_query, grad_key, grad_value, grad_outgate, grad_output = last[:5]
    return (
        hidden_out,
        grad_in[None],
        last[5][0],
        grad_query,
        grad_key,
        grad_value,
        grad_outgate,
        last[6].T,
        last[7],
        last[8][0],
        last[9][0],
        grad_output,
        last[10][0],
        grad_gate,
        grad_up,
        grad_down,
    )


def solution(mesh):
    sizes = dict(mesh.shape)
    cores = 2
    inner = Mesh(
        mesh.devices.reshape(sizes["dp"] // cores, cores, sizes["ctx"], sizes["tp"]),
        ("dpo", "core", "ctx", "tp"),
    )
    dp = ("dpo", "core")
    tokens = P(dp, ("ctx", "tp"), None)
    columns = P((*dp, "ctx"), "tp")
    rows = P("tp", (*dp, "ctx"))
    return jax.shard_map(
        on_device,
        mesh=inner,
        in_specs=(
            tokens,
            tokens,
            P(dp, None),
            P(),
            columns,
            columns,
            columns,
            columns,
            P(),
            P(),
            P(),
            P(),
            rows,
            P(),
            columns,
            columns,
            rows,
        ),
        out_specs=(
            tokens,
            tokens,
            P(),
            columns,
            columns,
            columns,
            columns,
            P(),
            P(),
            P(),
            P(),
            rows,
            P(),
            columns,
            columns,
            rows,
        ),
        check_vma=False,
    )
```
